256 devices in a mesh: ctx: 32 (over y_lo, z, core), slab: 8 (over x, y_hi).
Axes of the slice: x: 4, y: 4 (y_hi: 2, y_lo: 2; y = y_hi * 2 + y_lo), z: 8, core: 2. Of those that a mesh axis runs over, the one named last changes fastest.
Arguments:
- queries: bfloat16 [1024, 8192], P(('ctx', 'slab')), may hold values from -360 to 360
- block_lists: int32 [1024, 32], P(('ctx', 'slab')), may hold values from 0 to 63, all different within a row
- suffix_lengths: int32 [1024], P(('ctx', 'slab')), may hold values from 1 to 256, 131072 in all
- prompt_keys: bfloat16 [64, 1024, 512], P('ctx', 'slab'), may hold values from -6 to 6
- prompt_values: bfloat16 [64, 1024, 512], P('ctx', 'slab'), may hold values from -6 to 6
- suffix_keys: bfloat16 [1024, 256, 512], P(('ctx', 'slab')), may hold values from -6 to 6
- suffix_values: bfloat16 [1024, 256, 512], P(('ctx', 'slab')), may hold values from -6 to 6
Outputs:
- attended: bfloat16 [1024, 8192], P(('ctx', 'slab'))
The draws below stay inside these ranges and needn't reach their ends.
Inputs may be any that keep to these rules, and one draw needn't show every extreme that they name: `block_lists`: each row names 32 different blocks; every block is named by some row. `suffix_lengths`: some branch has exactly 256 suffix tokens.
All inputs are finite; a program needn't handle non-finite values. No bound on the sum of `suffix_lengths` on one device may be relied on, other than what follows from the above.
Results may differ from the reference program's by a relative error of at most 0.0166.
Values may be sent and summed in bfloat16 or wider, within the bound.
A program may use at most 128 MiB of HBM per device.

```python
import math
import jax
import jax.numpy as jnp
import numpy as np
from jax import lax

HEADS = 64
KV_HEADS = 4
HEAD_DIM = 128
SUF = 256
B = 1024
NBLK = 64
BLK = 1024
VIS = 32


def draw_queries(key, part):
    key = jax.random.fold_in(key, 11)
    base_key = jax.random.fold_in(key, 0)
    values = jnp.clip(jax.random.normal(base_key, (B, HEADS * HEAD_DIM), jnp.float32), -6.0, 6.0)
    return values.astype(jnp.bfloat16)


def block_levels(rng, extent, cuts, smallest, top_value):
    factor_of, own = 1.0, jax.random.fold_in(rng, 6)
    for position, shards_of in cuts:
        steps = jnp.exp(jax.random.uniform(jax.random.fold_in(own, position), (shards_of,), jnp.float32, smallest / len(cuts), top_value / len(cuts)))
        factor_of = factor_of * jnp.repeat(steps, extent[position] // shards_of).reshape([-1 if axis == position else 1 for axis in range(len(extent))])
    return factor_of


def choose_distinct(stream_key, rows, amount, top, lift):
    ranking = jax.random.permutation(jax.random.fold_in(stream_key, 1), amount)
    boost = ranking
    for power in range(3):
        boost = boost * boost // amount
    boost = boost * lift // amount
    lots = jax.random.randint(jax.random.fold_in(stream_key, 2), (rows, amount), 0, 4096) + boost
    sure = jax.random.permutation(jax.random.fold_in(stream_key, 3), rows)[jnp.arange(amount) % rows]
    lots = jnp.where(jnp.arange(rows)[:, None] == sure[None, :], 1 << 14, lots)
    merit = lots * amount + jnp.arange(amount)
    return lax.top_k(merit.astype(jnp.int32), top)[1].astype(jnp.int32)


def length_profile(count, total, reach, skew):
    portions = [(1 << 20) // math.isqrt(grade ** skew) + 1 for grade in range(2, count + 1)]
    surplus, holding = total - reach - (count - 1), [1] * (count - 1)
    while surplus > 0:
        movable = [i for i in range(count - 1) if holding[i] < reach]
        whole, remaining = sum([portions[i] for i in movable]), surplus
        for i in movable:
            extra = min(reach - holding[i], max(1, remaining * portions[i] // whole), surplus)
            holding[i] = holding[i] + extra
            surplus = surplus - extra
    return np.array([reach] + holding)


def uneven(key, amount, total, bound, slope):
    if amount == 2:
        one = jax.random.randint(key, (), max(1, total - bound), min(bound, total - 1) + 1)
        return jnp.stack([one, total - one])
    tallies = jnp.asarray(length_profile(amount, total, bound, slope), jnp.int32)
    couples = (amount - 1) // 2
    source_of, sink = tallies[1:1 + 2 * couples:2], tallies[2:2 + 2 * couples:2]
    slack = jnp.minimum(source_of - 1, bound - sink)
    passed = jax.random.randint(jax.random.fold_in(key, 1), (couples,), 0, 1 << 20) % (slack + 1)
    tallies = tallies.at[1:1 + 2 * couples:2].set(source_of - passed).at[2:2 + 2 * couples:2].set(sink + passed)
    return tallies[jax.random.permutation(jax.random.fold_in(key, 2), amount)]


def noise(rng, dims, deviation, bound, cuts=(), kind=jnp.bfloat16):
    values = deviation * jax.random.normal(rng, dims, jnp.float32)
    if cuts:
        values = values * block_levels(rng, dims, cuts, -0.22, 0.18)
    return jnp.clip(values, -bound, bound).astype(kind)


def setup_inputs(seed: int = 0) -> dict:
    splits = jax.random.split(jax.random.key(seed), 8)
    return {
        "queries": draw_queries(jax.random.fold_in(splits[7], 71), 0),
        "block_lists": choose_distinct(splits[1], B, NBLK, VIS, 8192),
        "suffix_lengths": uneven(splits[2], B, B * SUF // 2, SUF, 1).astype(jnp.int32),
        "prompt_keys": noise(splits[3], (NBLK, BLK, KV_HEADS * HEAD_DIM), 1.0, 6.0, ((0, 32), (1, 8))),
        "prompt_values": noise(splits[4], (NBLK, BLK, KV_HEADS * HEAD_DIM), 1.0, 6.0, ((0, 32), (1, 8))),
        "suffix_keys": noise(splits[5], (B, SUF, KV_HEADS * HEAD_DIM), 1.0, 6.0, ((0, 256),)),
        "suffix_values": noise(splits[6], (B, SUF, KV_HEADS * HEAD_DIM), 1.0, 6.0, ((0, 256),)),
    }


NEG = -1.0e30


def reference(queries, block_lists, suffix_lengths, prompt_keys, prompt_values, suffix_keys, suffix_values):
    score_scale = HEAD_DIM ** -0.5
    ratio = HEADS // KV_HEADS
    all_tokens = NBLK * BLK
    all_keys = prompt_keys.reshape(all_tokens, KV_HEADS, HEAD_DIM).astype(jnp.float32)
    all_values = prompt_values.reshape(all_tokens, KV_HEADS, HEAD_DIM).astype(jnp.float32)
    token_block = jnp.arange(all_tokens, dtype=jnp.int32) // BLK
    group_size = math.gcd(B, 32)
    groups = B // group_size

    def one_group(inputs):
        query_rows, branch_lists, lengths, own_keys, own_values = inputs
        query_heads = query_rows.reshape(group_size, KV_HEADS, ratio, HEAD_DIM).astype(jnp.float32)
        visible = jnp.any(branch_lists[:, :, None] == jnp.arange(NBLK, dtype=jnp.int32)[None, None, :], axis=1)
        usable = visible[:, token_block][:, None, None, :]
        scores = jnp.einsum('bgrd,tgd->bgrt', query_heads, all_keys) * score_scale
        suffix_heads = own_keys.reshape(group_size, SUF, KV_HEADS, HEAD_DIM).astype(jnp.float32)
        suffix_scores = jnp.einsum('bgrd,btgd->bgrt', query_heads, suffix_heads) * score_scale
        suffix_usable = (jnp.arange(SUF, dtype=jnp.int32)[None, :] < lengths[:, None])[:, None, None, :]
        row_top = jnp.maximum(jnp.max(jnp.where(usable, scores, NEG), axis=-1),
                              jnp.max(jnp.where(suffix_usable, suffix_scores, NEG), axis=-1))
        weights = jnp.where(usable, jnp.exp(scores - row_top[..., None]), 0.0)
        suffix_weights = jnp.where(suffix_usable, jnp.exp(suffix_scores - row_top[..., None]), 0.0)
        row_total = jnp.sum(weights, axis=-1) + jnp.sum(suffix_weights, axis=-1)
        rounded = lax.optimization_barrier(weights.astype(jnp.bfloat16)).astype(jnp.float32)
        suffix_rounded = lax.optimization_barrier(suffix_weights.astype(jnp.bfloat16)).astype(jnp.float32)
        value_heads = own_values.reshape(group_size, SUF, KV_HEADS, HEAD_DIM).astype(jnp.float32)
        summed = jnp.einsum('bgrt,tgd->bgrd', rounded, all_values) + jnp.einsum('bgrt,btgd->bgrd', suffix_rounded, value_heads)
        result = summed / row_total[..., None]
        return result.reshape(group_size, HEADS * HEAD_DIM).astype(jnp.bfloat16)

    outputs = lax.map(one_group, (queries.reshape(groups, group_size, HEADS * HEAD_DIM),
                                  block_lists.reshape(groups, group_size, VIS),
                                  suffix_lengths.reshape(groups, group_size),
                                  suffix_keys.reshape(groups, group_size, SUF, KV_HEADS * HEAD_DIM),
                                  suffix_values.reshape(groups, group_size, SUF, KV_HEADS * HEAD_DIM)))
    return outputs.reshape(B, HEADS * HEAD_DIM)
```

```python
import jax
import jax.numpy as jnp
from jax import lax
from jax.experimental import pallas as pl
from jax.experimental.pallas import tpu as pltpu
from jax.sharding import PartitionSpec as P

HEADS = 64
KV_HEADS = 4
HEAD_DIM = 128
RATIO = HEADS // KV_HEADS
NEG = -1e30
EXP_SCALE = 1.4426950408889634 / HEAD_DIM**0.5

NX, NY, NZ = 4, 4, 8
OWN = 4
ROWS = 64
QROWS = 144
PROWS = 144
COPIES = 192

NT = (((1,), (1,)), ((), ()))
TN = (((0,), (0,)), ((), ()))
f32 = jnp.float32
bf16 = jnp.bfloat16


def combine(a, b):
    top_a, top_b = a[128:129], b[128:129]
    top = jnp.maximum(top_a, top_b)
    fa = jnp.exp2((top_a - top) * EXP_SCALE)
    fb = jnp.exp2((top_b - top) * EXP_SCALE)
    values = a[:128] * fa + b[:128] * fb
    total = (a[129:130] + a[130:131]) * fa + (b[129:130] + b[130:131]) * fb
    return values, top, total


def pack(values, top, total):
    high = total.astype(bf16).astype(f32)
    row = lax.broadcasted_iota(jnp.int32, (16, values.shape[1]), 0)
    tail = jnp.where(row == 0, top, jnp.where(row == 1, high, jnp.where(row == 2, total - high, 0.0)))
    return jnp.concatenate([values.astype(bf16), tail.astype(bf16)], axis=0)


def kernel(
    q_hbm, list_hbm, len_in, k_hbm, v_hbm, sk_hbm, sv_hbm, out_ref,
    q_in, list_in, k_in, v_in, sk_in, sv_in, qfmt, work, bits_own, bits_sib,
    qbuf, kv, vsib, scores0, scores1, part, ra, rb, rc, rz1, rz0, ry0, swap, suf_o, suf_ml,
    send_sems, recv_sems, loc_sems,
):
    ctx = lax.axis_index("ctx")
    slab = lax.axis_index("slab")
    core = lax.rem(ctx, 2)
    z = lax.rem(ctx // 2, NZ)
    x = slab // 2
    y = lax.rem(slab, 2) * 2 + ctx // (2 * NZ)

    def device(x, y, z, core):
        return (lax.rem(y, 2) * NZ + z) * 2 + core, x * 2 + y // 2

    sib = device(x, y, z, 1 - core)
    xp = device(lax.rem(x + 1, NX), y, z, core)
    xm = device(lax.rem(x + NX - 1, NX), y, z, core)
    yp = device(x, lax.rem(y + 1, NY), z, core)
    ym = device(x, lax.rem(y + NY - 1, NY), z, core)
    zp = device(x, y, lax.rem(z + 1, NZ), core)
    zm = device(x, y, lax.rem(z + NZ - 1, NZ), core)

    loads = []
    pairs = ((q_hbm, q_in), (list_hbm, list_in), (k_hbm, k_in), (v_hbm, v_in), (sk_hbm, sk_in), (sv_hbm, sv_in))
    for n, (src, dst) in enumerate(pairs):
        loads.append(pltpu.make_async_copy(src, dst, loc_sems.at[n]))
        loads[n].start()

    barrier = pltpu.get_barrier_semaphore()
    for other in (sib, xp, xm, yp, ym, zp, zm):
        pl.semaphore_signal(barrier, inc=1, device_id=other, device_id_type=pl.DeviceIdType.MESH)

    loads[0].wait()
    for half in range(2):
        for k in range(2):
            for h in range(RATIO):
                col = ((half * 2 + k) * RATIO + h) * HEAD_DIM
                work[pl.ds(h * OWN, OWN), :] = q_in[:, col : col + HEAD_DIM].astype(f32)
            qfmt[half, k] = work[0:ROWS, :].astype(bf16)
    loads[1].wait()
    lists = list_in[...]
    lane = lax.broadcasted_iota(jnp.int32, (OWN, 128), 1)
    seen = jnp.zeros((OWN, 128), f32)
    for n in range(lists.shape[1]):
        seen = jnp.where(lists[:, n : n + 1] == lane, 1.0, seen)
    for dst, at in ((bits_own, 0), (bits_sib, OWN)):
        work[0:16, :] = jnp.zeros((16, 128), f32)
        work[pl.ds(at, OWN), :] = seen
        dst[0] = work[0:16, :].astype(bf16)

    pl.semaphore_wait(barrier, 7)

    copies = {}
    done = set()

    def send(name, src, dst, to):
        n = len(copies)
        copy = pltpu.make_async_remote_copy(
            src_ref=src, dst_ref=dst, send_sem=send_sems.at[n], recv_sem=recv_sems.at[n],
            device_id=to, device_id_type=pl.DeviceIdType.MESH,
        )
        copy.start()
        copies[name] = copy

    def got(*name):
        if name not in done:
            done.add(name)
            copies[name].wait_recv()

    send(("bits",), bits_sib.at[0], bits_sib.at[1], sib)
    for k in range(2):
        send(("qsib", k), qfmt.at[1 - core, k], qbuf.at[k, 0, 0, pl.ds(ROWS, ROWS)], sib)
        qbuf[k, 0, 0, 0:ROWS, :] = qfmt[core, k]

    def own_kv(k):
        mine = pl.ds(pl.multiple_of(core * 256 + k * 128, 128), 128)
        theirs = pl.ds(pl.multiple_of((1 - core) * 256 + k * 128, 128), 128)
        for blk in range(2):
            vsib[k, 0, blk] = k_in[blk, :, theirs]
            vsib[k, 1, blk] = v_in[blk, :, theirs].T
        send(("kvsib", k), vsib.at[k], kv.at[k, 0, 1], sib)
        for blk in range(2):
            kv[k, 0, 0, 0, blk] = k_in[blk, :, mine]
            kv[k, 0, 0, 1, blk] = v_in[blk, :, mine].T

    def kv_round(k, r):
        if r == 0:
            got("kvsib", k)
            send(("kv1", k), kv.at[k, 0], kv.at[k, 1], xp)
            send(("kv2", k), kv.at[k, 0], kv.at[k, 2], xm)
        elif r == 1:
            got("kv1", k)
            send(("kv3a", k), kv.at[k, 1, 0], kv.at[k, 3, 0], xp)
            got("kv2", k)
            send(("kv3b", k), kv.at[k, 2, 1], kv.at[k, 3, 1], xm)
        else:
            got("kv3a", k)
            got("kv3b", k)

    def slot(k, dy, dz, which):
        end = QROWS if k == 0 else 2 * ROWS
        first, last = ((0, end), (0, ROWS), (ROWS, end))[which]
        return qbuf.at[k, dy, dz, pl.ds(first, last - first)]

    def y_send(k, dz):
        send(("y3", k, dz), slot(k, 0, dz, 0), slot(k, 3, dz, 0), yp)
        send(("y1", k, dz), slot(k, 0, dz, 0), slot(k, 1, dz, 0), ym)

    def y_forward(k, dz):
        got("y3", k, dz)
        send(("y2a", k, dz), slot(k, 3, dz, 1), slot(k, 2, dz, 1), yp)
        got("y1", k, dz)
        send(("y2b", k, dz), slot(k, 1, dz, 2), slot(k, 2, dz, 2), ym)

    def z_send(k, s):
        if s <= 3:
            send(("z", k, NZ - s), slot(k, 0, (NZ + 1 - s) % NZ, 0), slot(k, 0, NZ - s, 0), zp)
            send(("z", k, s), slot(k, 0, s - 1, 0), slot(k, 0, s, 0), zm)
        else:
            send(("z4a", k), slot(k, 0, 5, 1), slot(k, 0, 4, 1), zp)
            send(("z4b", k), slot(k, 0, 3, 2), slot(k, 0, 4, 2), zm)

    def q_round(k, r):
        if r == 0:
            got("qsib", k)
            if k == 0:
                got("bits")
                qbuf[0, 0, 0, 2 * ROWS : QROWS, :] = bits_own[0] + bits_sib[1]
            z_send(k, 1)
            y_send(k, 0)
        elif r <= 3:
            got("z", k, NZ - r)
            got("z", k, r)
            z_send(k, r + 1)
            y_send(k, NZ - r)
            y_send(k, r)
        elif r == 4:
            got("z4a", k)
            got("z4b", k)
            y_send(k, 4)
        if r == 1:
            y_forward(k, 0)
        elif 2 <= r <= 4:
            y_forward(k, NZ - r + 1)
            y_forward(k, r - 1)
        elif r == 5:
            y_forward(k, 4)

    def need(k, dy, p):
        for dz in (2 * p, 2 * p + 1):
            if dy == 2:
                got("y2a", k, dz)
                got("y2b", k, dz)

    def suffix(k):
        zero = jnp.zeros((ROWS, 128), bf16)
        s = None
        for half in range(2):
            which = core if half == 0 else 1 - core
            cols = pl.ds(pl.multiple_of(which * 256 + k * 128, 128), 128)
            q = qfmt[which, k]
            q = jnp.concatenate([q, zero] if half == 0 else [zero, q], axis=0)
            keys = sk_in[:, :, cols].reshape(1024, 128)
            more = lax.dot_general(keys, q, NT, preferred_element_type=f32)
            s = more if s is None else s + more
        token = lax.broadcasted_iota(jnp.int32, (1024, 128), 0)
        lane = lax.broadcasted_iota(jnp.int32, (1024, 128), 1)
        branch = lax.broadcasted_iota(jnp.int32, (1, 128), 1) & (OWN - 1)
        length = jnp.zeros((1, 128), jnp.int32)
        for b in range(OWN):
            length = jnp.where(branch == b, len_in[b], length)
        ok = ((token >> 8) == (lane & (OWN - 1))) & ((token & 255) < length)
        top = jnp.max(jnp.where(ok, s, NEG), axis=0, keepdims=True)
        w = jnp.where(ok, jnp.exp2((s - top) * EXP_SCALE), 0.0)
        total = jnp.sum(w, axis=0, keepdims=True)
        w = w.astype(bf16)
        both = []
        for half in range(2):
            which = core if half == 0 else 1 - core
            cols = pl.ds(pl.multiple_of(which * 256 + k * 128, 128), 128)
            values = sv_in[:, :, cols].reshape(1024, 128)
            both.append(lax.dot_general(values, w, TN, preferred_element_type=f32))
        lane = lax.broadcasted_iota(jnp.int32, (128, 128), 1)
        suf_o[k] = jnp.where(lane < ROWS, both[0], both[1])
        suf_ml[k, 0:1] = top
        suf_ml[k, 1:2] = total

    row = lax.broadcasted_iota(jnp.int32, (8, 128), 0)
    lane = lax.broadcasted_iota(jnp.int32, (8, 128), 1)
    block_id = jnp.where(row < 2, 2 * ctx + row, 2 * (ctx + 1 - 2 * core) + row - 2)
    pick = ((lane == block_id) & (row < 4)).astype(f32).astype(bf16)
    row = lax.broadcasted_iota(jnp.int32, (32, 256), 0)
    lane = lax.broadcasted_iota(jnp.int32, (32, 256), 1)
    spread = ((row >> 4) == (lane >> 7)) & ((row & 15) == ((lane >> 6) & 1) * OWN + (lane & (OWN - 1)))
    spread = spread.astype(f32).astype(bf16)
    ones = jnp.ones((16, 512), bf16)

    class Tile:
        def __init__(self, n, k, dy, p):
            self.k, self.dy, self.p = k, dy, p
            self.scores = (scores0, scores1)[n % 2]
            need(k, dy, p)
            self.q = qbuf[k, dy, 2 * p : 2 * p + 2, 0 : 2 * ROWS, :].reshape(256, 128)
            bits = qbuf[0, dy, 2 * p : 2 * p + 2, 2 * ROWS : QROWS, :].reshape(32, 128)
            seen = lax.dot_general(pick, bits, NT, preferred_element_type=f32).astype(bf16)
            self.seen = jnp.dot(seen, spread, preferred_element_type=f32) > 0.5
            self.top = jnp.full((1, 256), NEG, f32)
            self.acc = jnp.zeros((PROWS, 256), f32)

        def front(self, j):
            keys = jnp.concatenate([kv[self.k, xs, j // 2, 0, j % 2] for xs in range(4)], axis=0)
            s = lax.dot_general(keys, self.q, NT, preferred_element_type=f32)
            self.scores[pl.ds(j * 512, 512), :] = s
            here = jnp.max(s, axis=0, keepdims=True)
            self.top = jnp.maximum(self.top, jnp.where(self.seen[j : j + 1], here, NEG))

        def back(self, j):
            if j == 0:
                self.top = self.top.astype(bf16).astype(f32)
            values = jnp.concatenate([kv[self.k, xs, j // 2, 1, j % 2] for xs in range(4)], axis=1)
            values = jnp.concatenate([values, ones], axis=0)
            shift = jnp.where(self.seen[j : j + 1], self.top, -NEG)
            w = jnp.exp2((self.scores[pl.ds(j * 512, 512), :] - shift) * EXP_SCALE).astype(bf16)
            self.acc = self.acc + jnp.dot(values, w, preferred_element_type=f32)

        def store(self):
            packed = pack(self.acc[:128], self.top, self.acc[128:129])
            part[self.k, self.dy, self.p * 2] = packed[:, :128]
            part[self.k, self.dy, self.p * 2 + 1] = packed[:, 128:]

    def merge(k, dy, dz, *others):
        total = part[k, dy, dz].astype(f32)
        for other in others[:-1]:
            values, top, mass = combine(total, other.astype(f32))
            row = lax.broadcasted_iota(jnp.int32, (16, 128), 0)
            tail = jnp.where(row == 0, top, jnp.where(row == 1, mass, 0.0))
            total = jnp.concatenate([values, tail], axis=0)
        part[k, dy, dz] = pack(*combine(total, others[-1].astype(f32)))

    def z0(s):
        near, far = 4 - s, 4 + s
        if s >= 1:
            got("z0p", s - 1)
            for dy in range(2 if s == 1 else 4):
                merge(0, dy, near, rz0[0, s - 1, dy])
            if s < 4:
                send(("z0p", s), part.at[0, pl.ds(0, 4), near], rz0.at[0, s], zp)
            got("z0m", s - 1)
            for dy in range(2 if s == 1 else 0, 4):
                merge(0, dy, far % NZ, rz0[1, s - 1, dy])
            if s < 4:
                send(("z0m", s), part.at[0, pl.ds(0, 4), far], rz0.at[1, s], zm)
        else:
            send(("z0p", 0), part.at[0, pl.ds(0, 2), 4], rz0.at[0, 0, pl.ds(0, 2)], zp)
            send(("z0m", 0), part.at[0, pl.ds(2, 2), 4], rz0.at[1, 0, pl.ds(2, 2)], zm)

    def y0(s):
        if s == 0:
            send(("y0a",), part.at[0, 2, 0], ry0.at[0], yp)
            send(("y0c",), part.at[0, 3, 0], ry0.at[2], ym)
        elif s == 1:
            got("y0a")
            merge(0, 1, 0, ry0[0])
            send(("y0b",), part.at[0, 1, 0], ry0.at[1], yp)
        else:
            got("y0b")
            got("y0c")
            merge(0, 0, 0, ry0[1], ry0[2])

    def y1(p, s):
        a, b = 2 * p, 2 * p + 1
        if s == 0:
            send(("ra", p), part.at[1, 2, a], ra.at[p], yp)
            send(("rb", p), part.at[1, 2, b], rb.at[p], ym)
        elif s == 1:
            send(("rcb", p), part.at[1, 1, b], rc.at[0, b], yp)
        elif s == 2:
            send(("rda", p), part.at[1, 3, a], rc.at[1, a], ym)
            got("ra", p)
            merge(1, 1, a, ra[p])
            send(("rca", p), part.at[1, 1, a], rc.at[0, a], yp)
            got("rb", p)
            merge(1, 3, b, rb[p])
            send(("rdb", p), part.at[1, 3, b], rc.at[1, b], ym)
        else:
            for name in ("rcb", "rda", "rca", "rdb"):
                got(name, p)
            merge(1, 0, a, rc[0, a], rc[1, a])
            merge(1, 0, b, rc[0, b], rc[1, b])

    def z1(dz):
        if dz in (3, 2, 1, 0):
            got("z1", dz + 1)
        if dz in (6, 7, 0):
            got("z1", 7 if dz == 0 else dz - 1)
        if dz == 0:
            merge(1, 0, 0, rz1[1], rz1[7])
            return
        if dz not in (4, 5):
            merge(1, 0, dz, rz1[dz + 1 if dz < 4 else dz - 1])
        send(("z1", dz), part.at[1, 0, dz], rz1.at[dz], zp if dz <= 4 else zm)

    def finish(k):
        got("swap", k)
        lane = lax.broadcasted_iota(jnp.int32, (PROWS, 128), 1)
        a = jnp.where(lane < ROWS, part[k, 0, 0].astype(f32), swap[k].astype(f32))
        top_a, top_b = a[128:129], suf_ml[k, 0:1]
        top = jnp.maximum(top_a, top_b)
        fa = jnp.exp2((top_a - top) * EXP_SCALE)
        fb = jnp.exp2((top_b - top) * EXP_SCALE)
        total = (a[129:130] + a[130:131]) * fa + suf_ml[k, 1:2] * fb
        work[...] = ((a[:128] * fa + suf_o[k] * fb) / total).T
        for half in range(2):
            which = core if half == 0 else 1 - core
            for h in range(RATIO):
                col = pl.multiple_of((which * 2 + k) * RATIO * HEAD_DIM + h * HEAD_DIM, 128)
                rows = work[pl.ds(half * ROWS + h * OWN, OWN), :]
                out_ref[:, pl.ds(col, HEAD_DIM)] = rows.astype(bf16)

    q_round(0, 0)
    loads[2].wait()
    loads[3].wait()
    own_kv(0)
    kv_round(0, 0)
    own_kv(1)
    q_round(0, 1)
    loads[4].wait()
    loads[5].wait()
    suffix(0)
    q_round(0, 2)
    kv_round(0, 1)
    q_round(0, 3)
    q_round(0, 4)
    suffix(1)
    q_round(0, 5)
    kv_round(0, 2)

    order = [(0, dy, p) for p in (0, 3, 1, 2) for dy in (0, 1, 3, 2)]
    order += [(1, dy, p) for p in (2, 1, 3, 0) for dy in (2, 1, 3, 0)]
    after = {}

    def at(n, f, *args):
        after.setdefault(n, []).append((f, args))

    kv_round(1, 0)
    q_round(1, 0)
    at(2, q_round, 1, 1)
    at(4, q_round, 1, 2)
    at(5, kv_round, 1, 1)
    at(6, q_round, 1, 3)
    at(8, q_round, 1, 4)
    at(10, q_round, 1, 5)
    at(13, kv_round, 1, 2)
    at(15, z0, 0)
    at(18, z0, 1)
    at(21, z0, 2)
    at(24, z0, 3)
    at(27, z0, 4)
    at(27, y0, 0)
    at(28, y0, 1)
    at(30, y0, 2)
    for i, p in enumerate((2, 1, 3, 0)):
        n = 16 + 4 * i
        at(n, y1, p, 0)
        at(n + 1, y1, p, 1)
        at(n + 2, y1, p, 2)
        at(n + 4 if i < 3 else n + 3, y1, p, 3)
    at(20, z1, 4)
    at(20, z1, 5)
    at(24, z1, 3)
    at(26, z1, 2)
    at(28, z1, 6)
    at(30, z1, 7)
    at(31, z1, 1)
    at(31, z1, 0)

    tile = Tile(0, *order[0])
    for j in range(4):
        tile.front(j)
    for n in range(len(order)):
        following = Tile(n + 1, *order[n + 1]) if n + 1 < len(order) else None
        for j in range(4):
            if following is not None:
                following.front(j)
            tile.back(j)
        tile.store()
        tile = following
        for f, args in after.get(n, []):
            f(*args)
    for k in range(2):
        send(("swap", k), part.at[k, 0, 0], swap.at[k], sib)
    for k in range(2):
        finish(k)
    for name, copy in copies.items():
        if name not in done:
            copy.wait_recv()
        copy.wait_send()


def shards(
    queries, block_lists, suffix_lengths, prompt_keys, prompt_values, suffix_keys, suffix_values
):
    hbm = pl.BlockSpec(memory_space=pltpu.HBM)
    vmem = pl.BlockSpec(memory_space=pltpu.VMEM)
    smem = pl.BlockSpec(memory_space=pltpu.SMEM)
    return pl.pallas_call(
        kernel,
        out_shape=jax.ShapeDtypeStruct(queries.shape, bf16),
        in_specs=[hbm, hbm, smem, hbm, hbm, hbm, hbm],
        out_specs=vmem,
        scratch_shapes=[
            pltpu.VMEM(queries.shape, bf16),
            pltpu.VMEM(block_lists.shape, jnp.int32),
            pltpu.VMEM(prompt_keys.shape, bf16),
            pltpu.VMEM(prompt_values.shape, bf16),
            pltpu.VMEM(suffix_keys.shape, bf16),
            pltpu.VMEM(suffix_values.shape, bf16),
            pltpu.VMEM((2, 2, ROWS, 128), bf16),
            pltpu.VMEM((128, 128), f32),
            pltpu.VMEM((1, 16, 128), bf16),
            pltpu.VMEM((2, 16, 128), bf16),
            pltpu.VMEM((2, NY, NZ, QROWS, 128), bf16),
            pltpu.VMEM((2, 4, 2, 2, 2, 128, 128), bf16),
            pltpu.VMEM((2, 2, 2, 128, 128), bf16),
            pltpu.VMEM((2048, 256), f32),
            pltpu.VMEM((2048, 256), f32),
            pltpu.VMEM((2, NY, NZ, PROWS, 128), bf16),
            pltpu.VMEM((4, PROWS, 128), bf16),
            pltpu.VMEM((4, PROWS, 128), bf16),
            pltpu.VMEM((2, NZ, PROWS, 128), bf16),
            pltpu.VMEM((NZ, PROWS, 128), bf16),
            pltpu.VMEM((2, 4, 4, PROWS, 128), bf16),
            pltpu.VMEM((3, PROWS, 128), bf16),
            pltpu.VMEM((2, PROWS, 128), bf16),
            pltpu.VMEM((2, 128, 128), f32),
            pltpu.VMEM((2, 8, 128), f32),
            pltpu.SemaphoreType.DMA((COPIES,)),
            pltpu.SemaphoreType.DMA((COPIES,)),
            pltpu.SemaphoreType.DMA((6,)),
        ],
        compiler_params=pltpu.CompilerParams(
            collective_id=0, has_side_effects=True, vmem_limit_bytes=56 * 1024 * 1024
        ),
    )(queries, block_lists, suffix_lengths, prompt_keys, prompt_values, suffix_keys, suffix_values)


def solution(mesh):
    return jax.shard_map(
        shards,
        mesh=mesh,
        in_specs=(
            P(("ctx", "slab"), None),
            P(("ctx", "slab"), None),
            P(("ctx", "slab")),
            P("ctx", "slab", None),
            P("ctx", "slab", None),
            P(("ctx", "slab"), None, None),
            P(("ctx", "slab"), None, None),
        ),
        out_specs=P(("ctx", "slab"), None),
        check_vma=False,
    )
```

```python
import jax
import jax.numpy as jnp
from jax import lax
from jax.experimental import pallas as pl
from jax.experimental.pallas import tpu as pltpu
from jax.sharding import PartitionSpec as P

HEADS = 64
KV_HEADS = 4
HEAD_DIM = 128
RATIO = HEADS // KV_HEADS
NEG = -1e30
EXP_SCALE = 1.4426950408889634 / HEAD_DIM**0.5

NX, NY, NZ = 4, 4, 8
OWN = 4
ROWS = 64
QROWS = 144
PROWS = 144
TILE = 512
COPIES = 192


def place(dz):
    return (dz + 1) % NZ


NT = (((1,), (1,)), ((), ()))
TN = (((0,), (0,)), ((), ()))
f32 = jnp.float32
bf16 = jnp.bfloat16


def combine(a, b):
    top_a, top_b = a[128:129], b[128:129]
    top = jnp.maximum(top_a, top_b)
    fa = jnp.exp2((top_a - top) * EXP_SCALE)
    fb = jnp.exp2((top_b - top) * EXP_SCALE)
    values = a[:128] * fa + b[:128] * fb
    total = (a[129:130] + a[130:131]) * fa + (b[129:130] + b[130:131]) * fb
    return values, top, total


def pack(values, top, total):
    high = total.astype(bf16).astype(f32)
    row = lax.broadcasted_iota(jnp.int32, (16, values.shape[1]), 0)
    tail = jnp.where(row == 0, top, jnp.where(row == 1, high, jnp.where(row == 2, total - high, 0.0)))
    return jnp.concatenate([values.astype(bf16), tail.astype(bf16)], axis=0)


def kernel(
    q_hbm, list_hbm, len_in, k_hbm, v_hbm, sk_hbm, sv_hbm, out_ref,
    q_in, list_in, k_in, v_in, sk_in, sv_in, qfmt, work, bits_own, bits_sib,
    qbuf, kv, vsib, scores0, scores1, hide, eye, part, ra, rb, rc, rz1, rz0, ry0, swap, suf_o, suf_ml,
    send_sems, recv_sems, loc_sems,
):
    ctx = lax.axis_index("ctx")
    slab = lax.axis_index("slab")
    core = lax.rem(ctx, 2)
    z = lax.rem(ctx // 2, NZ)
    x = slab // 2
    y = lax.rem(slab, 2) * 2 + ctx // (2 * NZ)

    def device(x, y, z, core):
        return (lax.rem(y, 2) * NZ + z) * 2 + core, x * 2 + y // 2

    sib = device(x, y, z, 1 - core)
    xp = device(lax.rem(x + 1, NX), y, z, core)
    xm = device(lax.rem(x + NX - 1, NX), y, z, core)
    yp = device(x, lax.rem(y + 1, NY), z, core)
    ym = device(x, lax.rem(y + NY - 1, NY), z, core)
    zp = device(x, y, lax.rem(z + 1, NZ), core)
    zm = device(x, y, lax.rem(z + NZ - 1, NZ), core)

    loads = []
    pairs = ((k_hbm, k_in), (v_hbm, v_in), (q_hbm, q_in), (list_hbm, list_in), (sk_hbm, sk_in), (sv_hbm, sv_in))
    for n, (src, dst) in enumerate(pairs):
        loads.append(pltpu.make_async_copy(src, dst, loc_sems.at[n]))
        loads[n].start()

    barrier = pltpu.get_barrier_semaphore()
    for other in (sib, xp, xm, yp, ym, zp, zm):
        pl.semaphore_signal(barrier, inc=1, device_id=other, device_id_type=pl.DeviceIdType.MESH)

    def own_kv(k):
        mine = pl.ds(pl.multiple_of(core * 256 + k * 128, 128), 128)
        theirs = pl.ds(pl.multiple_of((1 - core) * 256 + k * 128, 128), 128)
        for blk in range(2):
            vsib[k, 0, blk] = k_in[blk, :, theirs].T
            vsib[k, 1, blk] = v_in[blk, :, theirs]
            kv[k, 0, 0, 0, blk] = k_in[blk, :, mine].T
            kv[k, 0, 0, 1, blk] = v_in[blk, :, mine]

    loads[0].wait()
    loads[1].wait()
    own_kv(0)

    loads[2].wait()

    def queries(k):
        for half in range(2):
            for h in range(RATIO):
                col = ((half * 2 + k) * RATIO + h) * HEAD_DIM
                work[pl.ds(h * OWN, OWN), :] = q_in[:, col : col + HEAD_DIM].astype(f32)
            qfmt[half, k] = work[0:ROWS, :].astype(bf16)

    queries(0)
    loads[3].wait()
    lists = list_in[...]
    lane = lax.broadcasted_iota(jnp.int32, (OWN, 128), 1)
    seen = jnp.zeros((OWN, 128), f32)
    for n in range(lists.shape[1]):
        seen = jnp.where(lists[:, n : n + 1] == lane, 1.0, seen)
    for dst, first in ((bits_own, 0), (bits_sib, OWN)):
        work[0:16, :] = jnp.zeros((16, 128), f32)
        work[pl.ds(first, OWN), :] = seen
        dst[0] = work[0:16, :].astype(bf16)

    pl.semaphore_wait(barrier, 7)

    copies = {}
    done = set()

    def copy_of(name):
        n, src, dst, to = copies[name]
        return pltpu.make_async_remote_copy(
            src_ref=src, dst_ref=dst, send_sem=send_sems.at[n], recv_sem=recv_sems.at[n],
            device_id=to, device_id_type=pl.DeviceIdType.MESH,
        )

    def send(name, src, dst, to):
        copies[name] = (len(copies), src, dst, to)
        copy_of(name).start()

    def got(*name):
        if name not in done:
            done.add(name)
            copy_of(name).wait_recv()

    def exchange(k):
        send(("kvsib", k), vsib.at[k], kv.at[k, 0, 1], sib)
        send(("qsib", k), qfmt.at[1 - core, k], qbuf.at[k, 0, place(0), pl.ds(ROWS, ROWS)], sib)
        qbuf[k, 0, place(0), 0:ROWS, :] = qfmt[core, k]

    def kv_round(k, r):
        if r <= 1:
            if r == 1:
                got("kvsib", k)
            send(("kv1", k, r), kv.at[k, 0, r], kv.at[k, 1, r], xp)
            send(("kv2", k, r), kv.at[k, 0, r], kv.at[k, 2, r], xm)
        elif r == 2:
            got("kv1", k, 0)
            send(("kv3", k, 0), kv.at[k, 1, 0], kv.at[k, 3, 0], xp)
        elif r == 3:
            got("kv2", k, 1)
            send(("kv3", k, 1), kv.at[k, 2, 1], kv.at[k, 3, 1], xm)
        else:
            got("kv1", k, 1)
            got("kv2", k, 0)
            got("kv3", k, 0)
            got("kv3", k, 1)

    def slot(k, dy, dz, which):
        end = QROWS if k == 0 else 2 * ROWS
        first, last = ((0, end), (0, ROWS), (ROWS, end))[which]
        return qbuf.at[k, dy, place(dz), pl.ds(first, last - first)]

    def y_send(k, dz):
        send(("y3", k, dz), slot(k, 0, dz, 0), slot(k, 3, dz, 0), yp)
        send(("y1", k, dz), slot(k, 0, dz, 0), slot(k, 1, dz, 0), ym)

    def y_forward(k, dz):
        got("y3", k, dz)
        send(("y2a", k, dz), slot(k, 3, dz, 1), slot(k, 2, dz, 1), yp)
        got("y1", k, dz)
        send(("y2b", k, dz), slot(k, 1, dz, 2), slot(k, 2, dz, 2), ym)

    def z_send(k, s):
        if s <= 3:
            send(("z", k, NZ - s), slot(k, 0, (NZ + 1 - s) % NZ, 0), slot(k, 0, NZ - s, 0), zp)
            send(("z", k, s), slot(k, 0, s - 1, 0), slot(k, 0, s, 0), zm)
        else:
            send(("z4a", k), slot(k, 0, 5, 1), slot(k, 0, 4, 1), zp)
            send(("z4b", k), slot(k, 0, 3, 2), slot(k, 0, 4, 2), zm)

    def q_round(k, r):
        if r == 0:
            got("qsib", k)
            if k == 0:
                got("bits")
                qbuf[0, 0, place(0), 2 * ROWS : QROWS, :] = bits_own[0] + bits_sib[1]
            z_send(k, 1)
            y_send(k, 0)
        elif r <= 3:
            got("z", k, NZ - r)
            got("z", k, r)
            z_send(k, r + 1)
            y_send(k, NZ - r)
            y_send(k, r)
        elif r == 4:
            got("z4a", k)
            got("z4b", k)
            y_send(k, 4)
        if r == 1:
            y_forward(k, 0)
        elif 2 <= r <= 4:
            y_forward(k, NZ - r + 1)
            y_forward(k, r - 1)
        elif r == 5:
            y_forward(k, 4)

    def y_last(k):
        for dz in range(NZ):
            got("y2a", k, dz)
            got("y2b", k, dz)

    def suffix(k):
        zero = jnp.zeros((ROWS, 128), bf16)
        s = None
        for half in range(2):
            which = core if half == 0 else 1 - core
            cols = pl.ds(pl.multiple_of(which * 256 + k * 128, 128), 128)
            q = qfmt[which, k]
            q = jnp.concatenate([q, zero] if half == 0 else [zero, q], axis=0)
            keys = sk_in[:, :, cols].reshape(1024, 128)
            more = lax.dot_general(keys, q, NT, preferred_element_type=f32)
            s = more if s is None else s + more
        token = lax.broadcasted_iota(jnp.int32, (1024, 128), 0)
        lane = lax.broadcasted_iota(jnp.int32, (1024, 128), 1)
        branch = lax.broadcasted_iota(jnp.int32, (1, 128), 1) & (OWN - 1)
        length = jnp.zeros((1, 128), jnp.int32)
        for b in range(OWN):
            length = jnp.where(branch == b, len_in[b], length)
        ok = ((token >> 8) == (lane & (OWN - 1))) & ((token & 255) < length)
        top = jnp.max(jnp.where(ok, s, NEG), axis=0, keepdims=True)
        w = jnp.where(ok, jnp.exp2((s - top) * EXP_SCALE), 0.0)
        total = jnp.sum(w, axis=0, keepdims=True)
        w = w.astype(bf16)
        both = []
        for half in range(2):
            which = core if half == 0 else 1 - core
            cols = pl.ds(pl.multiple_of(which * 256 + k * 128, 128), 128)
            values = sv_in[:, :, cols].reshape(1024, 128)
            both.append(lax.dot_general(values, w, TN, preferred_element_type=f32))
        lane = lax.broadcasted_iota(jnp.int32, (128, 128), 1)
        suf_o[k] = jnp.where(lane < ROWS, both[0], both[1])
        suf_ml[k, 0:1] = top
        suf_ml[k, 1:2] = total

    row = lax.broadcasted_iota(jnp.int32, (128, 128), 0)
    lane = lax.broadcasted_iota(jnp.int32, (128, 128), 1)
    block_id = jnp.where(lane < 2, 2 * ctx + lane, 2 * (ctx + 1 - 2 * core) + lane - 2)
    pick = ((row == block_id) & (lane < 4)).astype(f32).astype(bf16)
    row = lax.broadcasted_iota(jnp.int32, (TILE, 64), 0)
    lane = lax.broadcasted_iota(jnp.int32, (TILE, 64), 1)
    spread = ((lane >> 4) == (row >> 7)) & ((lane & 15) == ((row >> 6) & 1) * OWN + (row & (OWN - 1)))
    spread = spread.astype(f32).astype(bf16)

    def constants():
        row = lax.broadcasted_iota(jnp.int32, (128, 128), 0)
        for j in range(4):
            hide[j] = jnp.where(row == j, NEG, 0.0).astype(bf16)
        row = lax.broadcasted_iota(jnp.int32, (PROWS, 256), 0)
        lane = lax.broadcasted_iota(jnp.int32, (PROWS, 256), 1)
        eye[...] = (row == lane).astype(f32).astype(bf16)

    class Tile:
        def __init__(self, n, k, dy, g):
            self.k, self.dy, self.slots = k, dy, pl.ds(4 * g, 4)
            self.scores = (scores0, scores1)[n % 2]

        def front(self, j):
            if j == 0:
                q = qbuf[self.k, self.dy, self.slots, 0 : 2 * ROWS, :].reshape(TILE, 128)
                bits = qbuf[0, self.dy, self.slots, 2 * ROWS : QROWS, :].reshape(64, 128)
                unseen = jnp.dot((1.0 - bits.astype(f32)).astype(bf16), pick, preferred_element_type=f32)
                unseen = jnp.dot(spread, unseen.astype(bf16), preferred_element_type=f32)
                self.q = jnp.concatenate([q, unseen.astype(bf16)], axis=1)
                self.top = jnp.full((TILE, 128), NEG, f32)
            keys = jnp.concatenate([kv[self.k, xs, j // 2, 0, j % 2] for xs in range(4)], axis=1)
            keys = jnp.concatenate([keys, jnp.concatenate([hide[j]] * 4, axis=1)], axis=0)
            s = jnp.dot(self.q, keys, preferred_element_type=f32)
            self.scores[:, pl.ds(j * 512, 512)] = s
            for c in range(0, 512, 128):
                self.top = jnp.maximum(self.top, s[:, c : c + 128])

        def back(self, j):
            if j == 0:
                top = jnp.max(self.top, axis=1, keepdims=True)
                self.top = jnp.maximum(top, 0.1 * NEG).astype(bf16).astype(f32)
                self.acc = jnp.zeros((TILE, 256), f32)
            values = jnp.concatenate([kv[self.k, xs, j // 2, 1, j % 2] for xs in range(4)], axis=0)
            values = jnp.concatenate([values, jnp.ones((512, 128), bf16)], axis=1)
            w = jnp.exp2((self.scores[:, pl.ds(j * 512, 512)] - self.top) * EXP_SCALE).astype(bf16)
            self.acc = self.acc + jnp.dot(w, values, preferred_element_type=f32)

        def store(self):
            total = self.acc[:, 128:]
            high = total.astype(bf16).astype(f32)
            lane = lax.broadcasted_iota(jnp.int32, (TILE, 128), 1)
            tail = jnp.where(lane == 0, self.top, jnp.where(lane == 1, high, jnp.where(lane == 2, total - high, 0.0)))
            packed = jnp.concatenate([self.acc[:, :128].astype(bf16), tail.astype(bf16)], axis=1)
            turned = lax.dot_general(eye[...], packed, NT, preferred_element_type=f32).astype(bf16)
            for i in range(4):
                part[self.k, self.dy, self.slots.start + i] = turned[:, i * 128 : i * 128 + 128]

    def merge(k, dy, dz, *others):
        dz = place(dz)
        others = [buf[tuple(index)] for buf, *index in others]
        total = part[k, dy, dz].astype(f32)
        for other in others[:-1]:
            values, top, mass = combine(total, other.astype(f32))
            row = lax.broadcasted_iota(jnp.int32, (16, 128), 0)
            tail = jnp.where(row == 0, top, jnp.where(row == 1, mass, 0.0))
            total = jnp.concatenate([values, tail], axis=0)
        part[k, dy, dz] = pack(*combine(total, others[-1].astype(f32)))

    def z0(s):
        near, far = 4 - s, 4 + s
        if s >= 1:
            got("z0p", s - 1)
            for dy in range(2 if s == 1 else 4):
                merge(0, dy, near, (rz0, 0, s - 1, dy))
            if s < 4:
                send(("z0p", s), part.at[0, pl.ds(0, 4), place(near)], rz0.at[0, s], zp)
            got("z0m", s - 1)
            for dy in range(2 if s == 1 else 0, 4):
                merge(0, dy, far % NZ, (rz0, 1, s - 1, dy))
            if s < 4:
                send(("z0m", s), part.at[0, pl.ds(0, 4), place(far)], rz0.at[1, s], zm)
        else:
            send(("z0p", 0), part.at[0, pl.ds(0, 2), place(4)], rz0.at[0, 0, pl.ds(0, 2)], zp)
            send(("z0m", 0), part.at[0, pl.ds(2, 2), place(4)], rz0.at[1, 0, pl.ds(2, 2)], zm)

    def y0(s):
        if s == 0:
            send(("y0a",), part.at[0, 2, place(0)], ry0.at[0], yp)
            send(("y0c",), part.at[0, 3, place(0)], ry0.at[2], ym)
        elif s == 1:
            got("y0a")
            merge(0, 1, 0, (ry0, 0))
            send(("y0b",), part.at[0, 1, place(0)], ry0.at[1], yp)
        else:
            got("y0b")
            got("y0c")
            merge(0, 0, 0, (ry0, 1), (ry0, 2))

    def y1(g, s):
        dzs = [(4 * g + i - 1) % NZ for i in range(4)]
        a, b = pl.ds(4 * g, 2), pl.ds(4 * g + 2, 2)
        if s == 0:
            send(("ra", g), part.at[1, 2, a], ra.at[g], yp)
            send(("rb", g), part.at[1, 2, b], rb.at[g], ym)
        elif s == 1:
            send(("rcb", g), part.at[1, 1, b], rc.at[0, b], yp)
        elif s == 2:
            send(("rda", g), part.at[1, 3, a], rc.at[1, a], ym)
            got("ra", g)
            for i in range(2):
                merge(1, 1, dzs[i], (ra, g, i))
            send(("rca", g), part.at[1, 1, a], rc.at[0, a], yp)
            got("rb", g)
            for i in range(2):
                merge(1, 3, dzs[2 + i], (rb, g, i))
            send(("rdb", g), part.at[1, 3, b], rc.at[1, b], ym)
        else:
            for name in ("rcb", "rda", "rca", "rdb"):
                got(name, g)
            for i in (1, 2, 0, 3) if g else (3, 0, 2, 1):
                merge(1, 0, dzs[i], (rc, 0, 4 * g + i), (rc, 1, 4 * g + i))

    def z1(dz):
        if dz in (3, 2, 1, 0):
            got("z1", dz + 1)
        if dz in (6, 7, 0):
            got("z1", 7 if dz == 0 else dz - 1)
        if dz == 0:
            merge(1, 0, 0, (rz1, 1), (rz1, 7))
            return
        if dz not in (4, 5):
            merge(1, 0, dz, (rz1, dz + 1 if dz < 4 else dz - 1))
        send(("z1", dz), part.at[1, 0, place(dz)], rz1.at[dz], zp if dz <= 4 else zm)

    def finish(k):
        got("swap", k)
        lane = lax.broadcasted_iota(jnp.int32, (PROWS, 128), 1)
        a = jnp.where(lane < ROWS, part[k, 0, place(0)].astype(f32), swap[k].astype(f32))
        top_a, top_b = a[128:129], suf_ml[k, 0:1]
        top = jnp.maximum(top_a, top_b)
        fa = jnp.exp2((top_a - top) * EXP_SCALE)
        fb = jnp.exp2((top_b - top) * EXP_SCALE)
        total = (a[129:130] + a[130:131]) * fa + suf_ml[k, 1:2] * fb
        work[...] = ((a[:128] * fa + suf_o[k] * fb) / total).T
        for half in range(2):
            which = core if half == 0 else 1 - core
            for h in range(RATIO):
                col = pl.multiple_of((which * 2 + k) * RATIO * HEAD_DIM + h * HEAD_DIM, 128)
                rows = work[pl.ds(half * ROWS + h * OWN, OWN), :]
                out_ref[:, pl.ds(col, HEAD_DIM)] = rows.astype(bf16)

    exchange(0)
    kv_round(0, 0)
    send(("bits",), bits_sib.at[0], bits_sib.at[1], sib)
    q_round(0, 0)
    kv_round(0, 1)
    own_kv(1)
    queries(1)
    constants()
    q_round(0, 1)
    loads[4].wait()
    loads[5].wait()
    suffix(0)
    q_round(0, 2)
    kv_round(0, 2)
    q_round(0, 3)
    q_round(0, 4)
    kv_round(0, 3)
    q_round(0, 5)
    exchange(1)
    suffix(1)
    kv_round(0, 4)
    kv_round(1, 0)
    q_round(1, 0)
    kv_round(1, 1)

    order = [(0, dy, g) for dy in (0, 1, 3, 2) for g in (0, 1)]
    order += [(1, dy, g) for g in (1, 0) for dy in (2, 1, 3, 0)]
    events = {}

    def at(n, f, *args):
        events.setdefault(n, []).append((f, args))

    at(0, q_round, 1, 1)
    at(1, q_round, 1, 2)
    at(1, kv_round, 1, 2)
    at(2, q_round, 1, 3)
    at(2, kv_round, 1, 3)
    at(3, q_round, 1, 4)
    at(4, q_round, 1, 5)
    at(4, y_last, 0)
    at(6, y_last, 1)
    at(6, kv_round, 1, 4)
    at(7, z0, 0)
    at(9, z0, 1)
    at(11, z0, 2)
    at(12, z0, 3)
    at(13, z0, 4)
    at(13, y0, 0)
    at(14, y0, 1)
    at(15, y0, 2)
    for i, g in enumerate((1, 0)):
        n = 8 + 4 * i
        at(n, y1, g, 0)
        at(n + 1, y1, g, 1)
        at(n + 2, y1, g, 2)
        at(n + 4 if i == 0 else n + 3, y1, g, 3)
    at(12, z1, 4)
    at(12, z1, 5)
    at(14, z1, 3)
    at(14, z1, 6)
    at(15, z1, 2)
    at(15, z1, 7)
    at(15, z1, 1)
    at(15, z1, 0)

    tile = Tile(0, *order[0])
    for j in range(4):
        tile.front(j)
    for n in range(len(order)):
        following = Tile(n + 1, *order[n + 1]) if n + 1 < len(order) else None
        for j in range(4):
            if following is not None:
                following.front(j)
            tile.back(j)
        tile.store()
        tile = following
        for f, args in events.get(n, []):
            f(*args)
    for k in range(2):
        send(("swap", k), part.at[k, 0, place(0)], swap.at[k], sib)
    for k in range(2):
        finish(k)
    for name in copies:
        if name not in done:
            copy_of(name).wait_recv()
        copy_of(name).wait_send()


def shards(
    queries, block_lists, suffix_lengths, prompt_keys, prompt_values, suffix_keys, suffix_values
):
    hbm = pl.BlockSpec(memory_space=pltpu.HBM)
    vmem = pl.BlockSpec(memory_space=pltpu.VMEM)
    smem = pl.BlockSpec(memory_space=pltpu.SMEM)
    return pl.pallas_call(
        kernel,
        out_shape=jax.ShapeDtypeStruct(queries.shape, bf16),
        in_specs=[hbm, hbm, smem, hbm, hbm, hbm, hbm],
        out_specs=vmem,
        scratch_shapes=[
            pltpu.VMEM(queries.shape, bf16),
            pltpu.VMEM(block_lists.shape, jnp.int32),
            pltpu.VMEM(prompt_keys.shape, bf16),
            pltpu.VMEM(prompt_values.shape, bf16),
            pltpu.VMEM(suffix_keys.shape, bf16),
            pltpu.VMEM(suffix_values.shape, bf16),
            pltpu.VMEM((2, 2, ROWS, 128), bf16),
            pltpu.VMEM((128, 128), f32),
            pltpu.VMEM((1, 16, 128), bf16),
            pltpu.VMEM((2, 16, 128), bf16),
            pltpu.VMEM((2, NY, NZ, QROWS, 128), bf16),
            pltpu.VMEM((2, 4, 2, 2, 2, 128, 128), bf16),
            pltpu.VMEM((2, 2, 2, 128, 128), bf16),
            pltpu.VMEM((TILE, 2048), f32),
            pltpu.VMEM((TILE, 2048), f32),
            pltpu.VMEM((4, 128, 128), bf16),
            pltpu.VMEM((PROWS, 256), bf16),
            pltpu.VMEM((2, NY, NZ, PROWS, 128), bf16),
            pltpu.VMEM((2, 2, PROWS, 128), bf16),
            pltpu.VMEM((2, 2, PROWS, 128), bf16),
            pltpu.VMEM((2, NZ, PROWS, 128), bf16),
            pltpu.VMEM((NZ, PROWS, 128), bf16),
            pltpu.VMEM((2, 4, 4, PROWS, 128), bf16),
            pltpu.VMEM((3, PROWS, 128), bf16),
            pltpu.VMEM((2, PROWS, 128), bf16),
            pltpu.VMEM((2, 128, 128), f32),
            pltpu.VMEM((2, 8, 128), f32),
            pltpu.SemaphoreType.DMA((COPIES,)),
            pltpu.SemaphoreType.DMA((COPIES,)),
            pltpu.SemaphoreType.DMA((6,)),
        ],
        compiler_params=pltpu.CompilerParams(
            collective_id=0, has_side_effects=True, vmem_limit_bytes=56 * 1024 * 1024
        ),
    )(queries, block_lists, suffix_lengths, prompt_keys, prompt_values, suffix_keys, suffix_values)


def solution(mesh):
    return jax.shard_map(
        shards,
        mesh=mesh,
        in_specs=(
            P(("ctx", "slab"), None),
            P(("ctx", "slab"), None),
            P(("ctx", "slab")),
            P("ctx", "slab", None),
            P("ctx", "slab", None),
            P(("ctx", "slab"), None, None),
            P(("ctx", "slab"), None, None),
        ),
        out_specs=P(("ctx", "slab"), None),
        check_vma=False,
    )
```

```python
import jax
import jax.numpy as jnp
from jax import lax
from jax.experimental import pallas as pl
from jax.experimental.pallas import tpu as pltpu
from jax.sharding import PartitionSpec as P

HEADS = 64
KV_HEADS = 4
HEAD_DIM = 128
RATIO = HEADS // KV_HEADS
NEG = -1e30
EXP_SCALE = 1.4426950408889634 / HEAD_DIM**0.5

NX, NY, NZ = 4, 4, 8
OWN = 4
ROWS = 64
QROWS = 272
PROWS = 144
COPIES = 192

NT = (((1,), (1,)), ((), ()))
TN = (((0,), (0,)), ((), ()))
f32 = jnp.float32
bf16 = jnp.bfloat16


def combine(a, b):
    top_a, top_b = a[128:129], b[128:129]
    top = jnp.maximum(top_a, top_b)
    fa = jnp.exp2((top_a - top) * EXP_SCALE)
    fb = jnp.exp2((top_b - top) * EXP_SCALE)
    values = a[:128] * fa + b[:128] * fb
    total = (a[129:130] + a[130:131]) * fa + (b[129:130] + b[130:131]) * fb
    return values, top, total


def pack(values, top, total):
    high = total.astype(bf16).astype(f32)
    row = lax.broadcasted_iota(jnp.int32, (16, values.shape[1]), 0)
    tail = jnp.where(row == 0, top, jnp.where(row == 1, high, jnp.where(row == 2, total - high, 0.0)))
    return jnp.concatenate([values.astype(bf16), tail.astype(bf16)], axis=0)


def position():
    ctx = lax.axis_index("ctx")
    slab = lax.axis_index("slab")
    core = lax.rem(ctx, 2)
    z = lax.rem(ctx // 2, NZ)
    x = slab // 2
    y = lax.rem(slab, 2) * 2 + ctx // (2 * NZ)

    def device(x, y, z, core):
        return (lax.rem(y, 2) * NZ + z) * 2 + core, x * 2 + y // 2

    sib = device(x, y, z, 1 - core)
    xp = device(lax.rem(x + 1, NX), y, z, core)
    xm = device(lax.rem(x + NX - 1, NX), y, z, core)
    yp = device(x, lax.rem(y + 1, NY), z, core)
    ym = device(x, lax.rem(y + NY - 1, NY), z, core)
    zp = device(x, y, lax.rem(z + 1, NZ), core)
    zm = device(x, y, lax.rem(z + NZ - 1, NZ), core)

    return ctx, core, sib, xp, xm, yp, ym, zp, zm


def sender(send_sems, recv_sems):
    copies = {}
    done = set()

    def send(name, src, dst, to):
        n = len(copies)
        copy = pltpu.make_async_remote_copy(
            src_ref=src, dst_ref=dst, send_sem=send_sems.at[n], recv_sem=recv_sems.at[n],
            device_id=to, device_id_type=pl.DeviceIdType.MESH,
        )
        copy.start()
        copies[name] = copy

    def got(*name):
        if name not in done:
            done.add(name)
            copies[name].wait_recv()

    def close():
        for name, copy in copies.items():
            if name not in done:
                copy.wait_recv()
            copy.wait_send()

    return send, got, close


def gather_kernel(
    q_hbm, list_hbm, len_in, k_hbm, v_hbm, sk_hbm, sv_hbm, q_out, kv_out, suf_o, suf_ml,
    q_in, list_in, k_in, v_in, sk_in, sv_in, qfmt, work, bits_own, bits_sib,
    qbuf, kv, vsib, send_sems, recv_sems, loc_sems,
):
    ctx, core, sib, xp, xm, yp, ym, zp, zm = position()
    loads = []
    pairs = ((q_hbm, q_in), (list_hbm, list_in), (k_hbm, k_in), (v_hbm, v_in), (sk_hbm, sk_in), (sv_hbm, sv_in))
    for n, (src, dst) in enumerate(pairs):
        loads.append(pltpu.make_async_copy(src, dst, loc_sems.at[n]))
        loads[n].start()

    barrier = pltpu.get_barrier_semaphore()
    for other in (sib, xp, xm, yp, ym, zp, zm):
        pl.semaphore_signal(barrier, inc=1, device_id=other, device_id_type=pl.DeviceIdType.MESH)

    loads[0].wait()
    for half in range(2):
        for k in range(2):
            for h in range(RATIO):
                col = ((half * 2 + k) * RATIO + h) * HEAD_DIM
                work[pl.ds(h * OWN, OWN), :] = q_in[:, col : col + HEAD_DIM].astype(f32)
            qfmt[half, k] = work[0:ROWS, :].astype(bf16)
    loads[1].wait()
    lists = list_in[...]
    lane = lax.broadcasted_iota(jnp.int32, (OWN, 128), 1)
    seen = jnp.zeros((OWN, 128), f32)
    for n in range(lists.shape[1]):
        seen = jnp.where(lists[:, n : n + 1] == lane, 1.0, seen)
    for dst, at in ((bits_own, 0), (bits_sib, OWN)):
        work[0:16, :] = jnp.zeros((16, 128), f32)
        work[pl.ds(at, OWN), :] = seen
        dst[0] = work[0:16, :].astype(bf16)

    pl.semaphore_wait(barrier, 7)

    send, got, close = sender(send_sems, recv_sems)

    send(("bits",), bits_sib.at[0], bits_sib.at[1], sib)
    for k in range(2):
        send(("qsib", k), qfmt.at[1 - core, k], qbuf.at[0, 0, pl.ds((2 * k + 1) * ROWS, ROWS)], sib)
        qbuf[0, 0, 2 * k * ROWS : (2 * k + 1) * ROWS, :] = qfmt[core, k]

    loads[2].wait()
    loads[3].wait()
    for k in range(2):
        mine = pl.ds(pl.multiple_of(core * 256 + k * 128, 128), 128)
        theirs = pl.ds(pl.multiple_of((1 - core) * 256 + k * 128, 128), 128)
        for blk in range(2):
            vsib[k, 0, blk] = k_in[blk, :, theirs]
            vsib[k, 1, blk] = v_in[blk, :, theirs].T
            kv[0, 0, k, 0, blk] = k_in[blk, :, mine]
            kv[0, 0, k, 1, blk] = v_in[blk, :, mine].T
    send(("kvsib",), vsib, kv.at[0, 1], sib)

    def kv_round(r):
        if r == 0:
            got("kvsib")
            send(("kv1",), kv.at[0], kv.at[1], xp)
            send(("kv2",), kv.at[0], kv.at[2], xm)
        elif r == 1:
            got("kv1")
            send(("kv3a",), kv.at[1, 0], kv.at[3, 0], xp)
            got("kv2")
            send(("kv3b",), kv.at[2, 1], kv.at[3, 1], xm)
        else:
            got("kv3a")
            got("kv3b")

    def slot(dy, dz, which):
        first, last = ((0, QROWS), (0, 2 * ROWS), (2 * ROWS, QROWS))[which]
        return qbuf.at[dy, dz, pl.ds(first, last - first)]

    def y_send(dz):
        send(("y3", dz), slot(0, dz, 0), slot(3, dz, 0), yp)
        send(("y1", dz), slot(0, dz, 0), slot(1, dz, 0), ym)

    def y_forward(dz):
        got("y3", dz)
        send(("y2a", dz), slot(3, dz, 1), slot(2, dz, 1), yp)
        got("y1", dz)
        send(("y2b", dz), slot(1, dz, 2), slot(2, dz, 2), ym)

    def z_send(s):
        if s <= 3:
            send(("z", NZ - s), slot(0, (NZ + 1 - s) % NZ, 0), slot(0, NZ - s, 0), zp)
            send(("z", s), slot(0, s - 1, 0), slot(0, s, 0), zm)
        else:
            send(("z4a",), slot(0, 5, 1), slot(0, 4, 1), zp)
            send(("z4b",), slot(0, 3, 2), slot(0, 4, 2), zm)

    def q_round(r):
        if r == 0:
            got("qsib", 0)
            got("qsib", 1)
            got("bits")
            qbuf[0, 0, 4 * ROWS : QROWS, :] = bits_own[0] + bits_sib[1]
            z_send(1)
            y_send(0)
        elif r <= 3:
            got("z", NZ - r)
            got("z", r)
            z_send(r + 1)
            y_send(NZ - r)
            y_send(r)
        elif r == 4:
            got("z4a")
            got("z4b")
            y_send(4)
        if r == 1:
            y_forward(0)
        elif 2 <= r <= 4:
            y_forward(NZ - r + 1)
            y_forward(r - 1)
        elif r == 5:
            y_forward(4)

    def suffix(k):
        zero = jnp.zeros((ROWS, 128), bf16)
        s = None
        for half in range(2):
            which = core if half == 0 else 1 - core
            cols = pl.ds(pl.multiple_of(which * 256 + k * 128, 128), 128)
            q = qfmt[which, k]
            q = jnp.concatenate([q, zero] if half == 0 else [zero, q], axis=0)
            keys = sk_in[:, :, cols].reshape(1024, 128)
            more = lax.dot_general(keys, q, NT, preferred_element_type=f32)
            s = more if s is None else s + more
        token = lax.broadcasted_iota(jnp.int32, (1024, 128), 0)
        lane = lax.broadcasted_iota(jnp.int32, (1024, 128), 1)
        branch = lax.broadcasted_iota(jnp.int32, (1, 128), 1) & (OWN - 1)
        length = jnp.zeros((1, 128), jnp.int32)
        for b in range(OWN):
            length = jnp.where(branch == b, len_in[b], length)
        ok = ((token >> 8) == (lane & (OWN - 1))) & ((token & 255) < length)
        top = jnp.max(jnp.where(ok, s, NEG), axis=0, keepdims=True)
        w = jnp.where(ok, jnp.exp2((s - top) * EXP_SCALE), 0.0)
        total = jnp.sum(w, axis=0, keepdims=True)
        w = w.astype(bf16)
        both = []
        for half in range(2):
            which = core if half == 0 else 1 - core
            cols = pl.ds(pl.multiple_of(which * 256 + k * 128, 128), 128)
            values = sv_in[:, :, cols].reshape(1024, 128)
            both.append(lax.dot_general(values, w, TN, preferred_element_type=f32))
        lane = lax.broadcasted_iota(jnp.int32, (128, 128), 1)
        suf_o[k] = jnp.where(lane < ROWS, both[0], both[1])
        suf_ml[k, 0:1] = top
        suf_ml[k, 1:2] = total

    q_round(0)
    kv_round(0)
    q_round(1)
    q_round(2)
    loads[4].wait()
    loads[5].wait()
    suffix(0)
    q_round(3)
    kv_round(1)
    q_round(4)
    suffix(1)
    q_round(5)
    kv_round(2)
    close()
    stores = [
        pltpu.make_async_copy(qbuf, q_out, loc_sems.at[0]),
        pltpu.make_async_copy(kv, kv_out, loc_sems.at[1]),
    ]
    for copy in stores:
        copy.start()
    for copy in stores:
        copy.wait()


def attend_kernel(
    q_hbm, kv_hbm, suf_o, suf_ml, out_ref,
    qbuf, kv, work, scores0, scores1, part, ra, rb, rc, rz1, rz0, ry0, swap, send_sems, recv_sems, loc_sems,
):
    ctx, core, sib, xp, xm, yp, ym, zp, zm = position()
    loads = [
        pltpu.make_async_copy(q_hbm, qbuf, loc_sems.at[0]),
        pltpu.make_async_copy(kv_hbm, kv, loc_sems.at[1]),
    ]
    for copy in loads:
        copy.start()
    barrier = pltpu.get_barrier_semaphore()
    for other in (sib, yp, ym, zp, zm):
        pl.semaphore_signal(barrier, inc=1, device_id=other, device_id_type=pl.DeviceIdType.MESH)
    send, got, close = sender(send_sems, recv_sems)
    for copy in loads:
        copy.wait()

    row = lax.broadcasted_iota(jnp.int32, (8, 128), 0)
    lane = lax.broadcasted_iota(jnp.int32, (8, 128), 1)
    block_id = jnp.where(row < 2, 2 * ctx + row, 2 * (ctx + 1 - 2 * core) + row - 2)
    pick = ((lane == block_id) & (row < 4)).astype(f32).astype(bf16)
    row = lax.broadcasted_iota(jnp.int32, (32, 256), 0)
    lane = lax.broadcasted_iota(jnp.int32, (32, 256), 1)
    spread = ((row >> 4) == (lane >> 7)) & ((row & 15) == ((lane >> 6) & 1) * OWN + (lane & (OWN - 1)))
    spread = spread.astype(f32).astype(bf16)
    ones = jnp.ones((16, 512), bf16)

    class Tile:
        def __init__(self, n, k, dy, p):
            self.k, self.dy, self.p = k, dy, p
            self.scores = (scores0, scores1)[n % 2]
            self.q = qbuf[dy, 2 * p : 2 * p + 2, 2 * k * ROWS : 2 * (k + 1) * ROWS, :].reshape(256, 128)
            bits = qbuf[dy, 2 * p : 2 * p + 2, 4 * ROWS : QROWS, :].reshape(32, 128)
            seen = lax.dot_general(pick, bits, NT, preferred_element_type=f32).astype(bf16)
            self.seen = jnp.dot(seen, spread, preferred_element_type=f32) > 0.5
            self.top = jnp.full((1, 256), NEG, f32)
            self.acc = jnp.zeros((PROWS, 256), f32)

        def front(self, j):
            keys = jnp.concatenate([kv[xs, j // 2, self.k, 0, j % 2] for xs in range(4)], axis=0)
            s = lax.dot_general(keys, self.q, NT, preferred_element_type=f32)
            self.scores[pl.ds(j * 512, 512), :] = s
            here = jnp.max(s, axis=0, keepdims=True)
            self.top = jnp.maximum(self.top, jnp.where(self.seen[j : j + 1], here, NEG))

        def back(self, j):
            if j == 0:
                self.top = self.top.astype(bf16).astype(f32)
            values = jnp.concatenate([kv[xs, j // 2, self.k, 1, j % 2] for xs in range(4)], axis=1)
            values = jnp.concatenate([values, ones], axis=0)
            shift = jnp.where(self.seen[j : j + 1], self.top, -NEG)
            w = jnp.exp2((self.scores[pl.ds(j * 512, 512), :] - shift) * EXP_SCALE).astype(bf16)
            self.acc = self.acc + jnp.dot(values, w, preferred_element_type=f32)

        def store(self):
            packed = pack(self.acc[:128], self.top, self.acc[128:129])
            part[self.k, self.dy, self.p * 2] = packed[:, :128]
            part[self.k, self.dy, self.p * 2 + 1] = packed[:, 128:]

    def merge(k, dy, dz, *others):
        total = part[k, dy, dz].astype(f32)
        for other in others[:-1]:
            values, top, mass = combine(total, other.astype(f32))
            row = lax.broadcasted_iota(jnp.int32, (16, 128), 0)
            tail = jnp.where(row == 0, top, jnp.where(row == 1, mass, 0.0))
            total = jnp.concatenate([values, tail], axis=0)
        part[k, dy, dz] = pack(*combine(total, others[-1].astype(f32)))

    def z0(s):
        near, far = 4 - s, 4 + s
        if s >= 1:
            got("z0p", s - 1)
            for dy in range(2 if s == 1 else 4):
                merge(0, dy, near, rz0[0, s - 1, dy])
            if s < 4:
                send(("z0p", s), part.at[0, pl.ds(0, 4), near], rz0.at[0, s], zp)
            got("z0m", s - 1)
            for dy in range(2 if s == 1 else 0, 4):
                merge(0, dy, far % NZ, rz0[1, s - 1, dy])
            if s < 4:
                send(("z0m", s), part.at[0, pl.ds(0, 4), far], rz0.at[1, s], zm)
        else:
            send(("z0p", 0), part.at[0, pl.ds(0, 2), 4], rz0.at[0, 0, pl.ds(0, 2)], zp)
            send(("z0m", 0), part.at[0, pl.ds(2, 2), 4], rz0.at[1, 0, pl.ds(2, 2)], zm)

    def y0(s):
        if s == 0:
            send(("y0a",), part.at[0, 2, 0], ry0.at[0], yp)
            send(("y0c",), part.at[0, 3, 0], ry0.at[2], ym)
        elif s == 1:
            got("y0a")
            merge(0, 1, 0, ry0[0])
            send(("y0b",), part.at[0, 1, 0], ry0.at[1], yp)
        else:
            got("y0b")
            got("y0c")
            merge(0, 0, 0, ry0[1], ry0[2])

    def y1(p, s):
        a, b = 2 * p, 2 * p + 1
        if s == 0:
            send(("ra", p), part.at[1, 2, a], ra.at[p], yp)
            send(("rb", p), part.at[1, 2, b], rb.at[p], ym)
        elif s == 1:
            send(("rcb", p), part.at[1, 1, b], rc.at[0, b], yp)
        elif s == 2:
            send(("rda", p), part.at[1, 3, a], rc.at[1, a], ym)
            got("ra", p)
            merge(1, 1, a, ra[p])
            send(("rca", p), part.at[1, 1, a], rc.at[0, a], yp)
            got("rb", p)
            merge(1, 3, b, rb[p])
            send(("rdb", p), part.at[1, 3, b], rc.at[1, b], ym)
        else:
            for name in ("rcb", "rda", "rca", "rdb"):
                got(name, p)
            merge(1, 0, a, rc[0, a], rc[1, a])
            merge(1, 0, b, rc[0, b], rc[1, b])

    def z1(dz):
        if dz in (3, 2, 1, 0):
            got("z1", dz + 1)
        if dz in (6, 7, 0):
            got("z1", 7 if dz == 0 else dz - 1)
        if dz == 0:
            merge(1, 0, 0, rz1[1], rz1[7])
            return
        if dz not in (4, 5):
            merge(1, 0, dz, rz1[dz + 1 if dz < 4 else dz - 1])
        send(("z1", dz), part.at[1, 0, dz], rz1.at[dz], zp if dz <= 4 else zm)

    def finish(k):
        got("swap", k)
        lane = lax.broadcasted_iota(jnp.int32, (PROWS, 128), 1)
        a = jnp.where(lane < ROWS, part[k, 0, 0].astype(f32), swap[k].astype(f32))
        top_a, top_b = a[128:129], suf_ml[k, 0:1]
        top = jnp.maximum(top_a, top_b)
        fa = jnp.exp2((top_a - top) * EXP_SCALE)
        fb = jnp.exp2((top_b - top) * EXP_SCALE)
        total = (a[129:130] + a[130:131]) * fa + suf_ml[k, 1:2] * fb
        work[...] = ((a[:128] * fa + suf_o[k] * fb) / total).T
        for half in range(2):
            which = core if half == 0 else 1 - core
            for h in range(RATIO):
                col = pl.multiple_of((which * 2 + k) * RATIO * HEAD_DIM + h * HEAD_DIM, 128)
                rows = work[pl.ds(half * ROWS + h * OWN, OWN), :]
                out_ref[:, pl.ds(col, HEAD_DIM)] = rows.astype(bf16)

    order = [(0, dy, p) for p in (0, 3, 1, 2) for dy in (0, 1, 3, 2)]
    order += [(1, dy, p) for p in (2, 1, 3, 0) for dy in (2, 1, 3, 0)]
    after = {}

    def at(n, f, *args):
        after.setdefault(n, []).append((f, args))

    at(15, z0, 0)
    at(18, z0, 1)
    at(21, z0, 2)
    at(24, z0, 3)
    at(27, z0, 4)
    at(27, y0, 0)
    at(28, y0, 1)
    at(30, y0, 2)
    for i, p in enumerate((2, 1, 3, 0)):
        n = 16 + 4 * i
        at(n, y1, p, 0)
        at(n + 1, y1, p, 1)
        at(n + 2, y1, p, 2)
        at(n + 4 if i < 3 else n + 3, y1, p, 3)
    at(20, z1, 4)
    at(20, z1, 5)
    at(24, z1, 3)
    at(26, z1, 2)
    at(28, z1, 6)
    at(30, z1, 7)
    at(31, z1, 1)
    at(31, z1, 0)

    tile = Tile(0, *order[0])
    for j in range(4):
        tile.front(j)
    for n in range(len(order)):
        following = Tile(n + 1, *order[n + 1]) if n + 1 < len(order) else None
        for j in range(4):
            if following is not None:
                following.front(j)
            tile.back(j)
        tile.store()
        tile = following
        if n == 14:
            pl.semaphore_wait(barrier, 5)
        for f, args in after.get(n, []):
            f(*args)
    for k in range(2):
        send(("swap", k), part.at[k, 0, 0], swap.at[k], sib)
    for k in range(2):
        finish(k)
    close()


def shards(
    queries, block_lists, suffix_lengths, prompt_keys, prompt_values, suffix_keys, suffix_values
):
    hbm = pl.BlockSpec(memory_space=pltpu.HBM)
    vmem = pl.BlockSpec(memory_space=pltpu.VMEM)
    smem = pl.BlockSpec(memory_space=pltpu.SMEM)
    q_shape, kv_shape = (NY, NZ, QROWS, 128), (4, 2, 2, 2, 2, 128, 128)
    gathered = pl.pallas_call(
        gather_kernel,
        out_shape=[
            jax.ShapeDtypeStruct(q_shape, bf16),
            jax.ShapeDtypeStruct(kv_shape, bf16),
            jax.ShapeDtypeStruct((2, 128, 128), f32),
            jax.ShapeDtypeStruct((2, 8, 128), f32),
        ],
        in_specs=[hbm, hbm, smem, hbm, hbm, hbm, hbm],
        out_specs=[hbm, hbm, vmem, vmem],
        scratch_shapes=[
            pltpu.VMEM(queries.shape, bf16),
            pltpu.VMEM(block_lists.shape, jnp.int32),
            pltpu.VMEM(prompt_keys.shape, bf16),
            pltpu.VMEM(prompt_values.shape, bf16),
            pltpu.VMEM(suffix_keys.shape, bf16),
            pltpu.VMEM(suffix_values.shape, bf16),
            pltpu.VMEM((2, 2, ROWS, 128), bf16),
            pltpu.VMEM((128, 128), f32),
            pltpu.VMEM((1, 16, 128), bf16),
            pltpu.VMEM((2, 16, 128), bf16),
            pltpu.VMEM(q_shape, bf16),
            pltpu.VMEM(kv_shape, bf16),
            pltpu.VMEM((2, 2, 2, 128, 128), bf16),
            pltpu.SemaphoreType.DMA((COPIES,)),
            pltpu.SemaphoreType.DMA((COPIES,)),
            pltpu.SemaphoreType.DMA((6,)),
        ],
        compiler_params=pltpu.CompilerParams(
            collective_id=0, has_side_effects=True, vmem_limit_bytes=56 * 1024 * 1024
        ),
    )(queries, block_lists, suffix_lengths, prompt_keys, prompt_values, suffix_keys, suffix_values)
    return pl.pallas_call(
        attend_kernel,
        out_shape=jax.ShapeDtypeStruct(queries.shape, bf16),
        in_specs=[hbm, hbm, vmem, vmem],
        out_specs=vmem,
        scratch_shapes=[
            pltpu.VMEM(q_shape, bf16),
            pltpu.VMEM(kv_shape, bf16),
            pltpu.VMEM((128, 128), f32),
            pltpu.VMEM((2048, 256), f32),
            pltpu.VMEM((2048, 256), f32),
            pltpu.VMEM((2, NY, NZ, PROWS, 128), bf16),
            pltpu.VMEM((4, PROWS, 128), bf16),
            pltpu.VMEM((4, PROWS, 128), bf16),
            pltpu.VMEM((2, NZ, PROWS, 128), bf16),
            pltpu.VMEM((NZ, PROWS, 128), bf16),
            pltpu.VMEM((2, 4, 4, PROWS, 128), bf16),
            pltpu.VMEM((3, PROWS, 128), bf16),
            pltpu.VMEM((2, PROWS, 128), bf16),
            pltpu.SemaphoreType.DMA((COPIES,)),
            pltpu.SemaphoreType.DMA((COPIES,)),
            pltpu.SemaphoreType.DMA((2,)),
        ],
        compiler_params=pltpu.CompilerParams(
            collective_id=1, has_side_effects=True, vmem_limit_bytes=56 * 1024 * 1024
        ),
    )(*gathered)


def solution(mesh):
    return jax.shard_map(
        shards,
        mesh=mesh,
        in_specs=(
            P(("ctx", "slab"), None),
            P(("ctx", "slab"), None),
            P(("ctx", "slab")),
            P("ctx", "slab", None),
            P("ctx", "slab", None),
            P(("ctx", "slab"), None, None),
            P(("ctx", "slab"), None, None),
        ),
        out_specs=P(("ctx", "slab"), None),
        check_vma=False,
    )
```

```python
import jax
import jax.numpy as jnp
from jax import lax
from jax.experimental import pallas as pl
from jax.experimental.pallas import tpu as pltpu
from jax.sharding import PartitionSpec as P

HEADS = 64
KV_HEADS = 4
HEAD_DIM = 128
RATIO = HEADS // KV_HEADS
NEG = -1e30
EXP_SCALE = 1.4426950408889634 / HEAD_DIM**0.5

NX, NY, NZ = 4, 4, 8
OWN = 4
ROWS = 64
QROWS = 80
PROWS = 144
TILE = 1024
COPIES = 192


def place(dz):
    return (dz + 1) % NZ


NT = (((1,), (1,)), ((), ()))
TN = (((0,), (0,)), ((), ()))
f32 = jnp.float32
bf16 = jnp.bfloat16


def combine(a, b):
    top_a, top_b = a[128:129], b[128:129]
    top = jnp.maximum(top_a, top_b)
    fa = jnp.exp2((top_a - top) * EXP_SCALE)
    fb = jnp.exp2((top_b - top) * EXP_SCALE)
    values = a[:128] * fa + b[:128] * fb
    total = (a[129:130] + a[130:131]) * fa + (b[129:130] + b[130:131]) * fb
    return values, top, total


def pack(values, top, total):
    high = total.astype(bf16).astype(f32)
    row = lax.broadcasted_iota(jnp.int32, (16, values.shape[1]), 0)
    tail = jnp.where(row == 0, top, jnp.where(row == 1, high, jnp.where(row == 2, total - high, 0.0)))
    return jnp.concatenate([values.astype(bf16), tail.astype(bf16)], axis=0)


def kernel(
    q_hbm, list_hbm, len_in, k_hbm, v_hbm, sk_hbm, sv_hbm, out_ref,
    q_in, list_in, k_in, v_in, sk_in, sv_in, qfmt, work,
    qbuf, kv, vsib, scores0, scores1, hide, eye, part, ra, rb, rc, fin, suf_o, suf_ml,
    send_sems, recv_sems, loc_sems,
):
    ctx = lax.axis_index("ctx")
    slab = lax.axis_index("slab")
    core = lax.rem(ctx, 2)
    z = lax.rem(ctx // 2, NZ)
    x = slab // 2
    y = lax.rem(slab, 2) * 2 + ctx // (2 * NZ)

    def device(x, y, z, core):
        return (lax.rem(y, 2) * NZ + z) * 2 + core, x * 2 + y // 2

    sib = device(x, y, z, 1 - core)
    xps = [device(lax.rem(x + 1, NX), y, z, c) for c in (core, 1 - core)]
    xms = [device(lax.rem(x + NX - 1, NX), y, z, c) for c in (core, 1 - core)]
    yp = device(x, lax.rem(y + 1, NY), z, core)
    ym = device(x, lax.rem(y + NY - 1, NY), z, core)
    along_z = [[device(x, y, lax.rem(z + dz, NZ), c) for dz in range(NZ)] for c in (core, 1 - core)]

    loads = []
    pairs = ((k_hbm, k_in), (v_hbm, v_in), (q_hbm, q_in), (list_hbm, list_in), (sk_hbm, sk_in), (sv_hbm, sv_in))
    for n, (src, dst) in enumerate(pairs):
        loads.append(pltpu.make_async_copy(src, dst, loc_sems.at[n]))
        loads[n].start()

    barrier = pltpu.get_barrier_semaphore()
    peers = [sib, *xps, *xms, yp, ym] + along_z[0][1:] + along_z[1][1:]
    for other in peers:
        pl.semaphore_signal(barrier, inc=1, device_id=other, device_id_type=pl.DeviceIdType.MESH)

    def own_kv(k):
        mine = pl.ds(pl.multiple_of(core * 256 + k * 128, 128), 128)
        theirs = pl.ds(pl.multiple_of((1 - core) * 256 + k * 128, 128), 128)
        for blk in range(2):
            vsib[k, 0, blk] = k_in[blk, :, theirs].T
            vsib[k, 1, blk] = v_in[blk, :, theirs]
            kv[k, 0, 0, 0, blk] = k_in[blk, :, mine].T
            kv[k, 0, 0, 1, blk] = v_in[blk, :, mine]

    loads[0].wait()
    loads[1].wait()
    own_kv(0)

    loads[2].wait()

    def queries(k):
        for half in range(2):
            for h in range(RATIO):
                col = ((half * 2 + k) * RATIO + h) * HEAD_DIM
                work[pl.ds(h * OWN, OWN), :] = q_in[:, col : col + HEAD_DIM].astype(f32)
            qfmt[half, k, 0:ROWS, :] = work[0:ROWS, :].astype(bf16)

    queries(0)
    loads[3].wait()
    lists = list_in[...]
    lane = lax.broadcasted_iota(jnp.int32, (OWN, 128), 1)
    seen = jnp.zeros((OWN, 128), f32)
    for n in range(lists.shape[1]):
        seen = jnp.where(lists[:, n : n + 1] == lane, 1.0, seen)
    work[0:16, :] = jnp.zeros((16, 128), f32)
    work[0:OWN, :] = seen
    for half in range(2):
        qfmt[half, 0, ROWS:QROWS, :] = work[0:16, :].astype(bf16)

    pl.semaphore_wait(barrier, len(peers))

    copies = {}
    done = set()

    def copy_of(name):
        n, src, dst, to = copies[name]
        return pltpu.make_async_remote_copy(
            src_ref=src, dst_ref=dst, send_sem=send_sems.at[n], recv_sem=recv_sems.at[n],
            device_id=to, device_id_type=pl.DeviceIdType.MESH,
        )

    def send(name, src, dst, to):
        copies[name] = (len(copies), src, dst, to)
        copy_of(name).start()

    def got(*name):
        if name not in done:
            done.add(name)
            copy_of(name).wait_recv()

    def kv_send(k):
        send(("kvsib", k), vsib.at[k], kv.at[k, 0, 1], sib)
        for c, src in enumerate((kv.at[k, 0, 0], vsib.at[k])):
            send(("kv1", k, c), src, kv.at[k, 1, c], xps[c])
            send(("kv2", k, c), src, kv.at[k, 2, c], xms[c])

    def kv_forward(k):
        got("kv1", k, 0)
        send(("kv3", k, 0), kv.at[k, 1, 0], kv.at[k, 3, 0], xps[0])
        got("kv2", k, 1)
        send(("kv3", k, 1), kv.at[k, 2, 1], kv.at[k, 3, 1], xms[0])

    def kv_last(k):
        got("kvsib", k)
        for c in range(2):
            for name in ("kv1", "kv2", "kv3"):
                got(name, k, c)

    def slot(k, dy, dz, which):
        rows = pl.ds(0, QROWS if k == 0 else ROWS)
        if which == 2:
            return qbuf.at[k, dy, place(dz), pl.ds(0, 2), rows]
        return qbuf.at[k, dy, place(dz), which, rows]

    def q_send(k):
        end = QROWS if k == 0 else ROWS
        qbuf[k, 0, place(0), 0, 0:end, :] = qfmt[core, k, 0:end, :]
        for to in (0, 1, 7, 2, 6, 3, 5, 4):
            for half in range(2):
                if to or half:
                    src = qfmt.at[core if half == 0 else 1 - core, k, pl.ds(0, end)]
                    send(("q", k, half, -to % NZ), src, slot(k, 0, -to, half), along_z[half][to])

    def y_send(k, *dzs):
        for dz in dzs:
            for half in range(2):
                if dz or half:
                    got("q", k, half, dz)
            send(("y3", k, dz), slot(k, 0, dz, 2), slot(k, 3, dz, 2), yp)
            send(("y1", k, dz), slot(k, 0, dz, 2), slot(k, 1, dz, 2), ym)

    def y_forward(k, *dzs):
        for dz in dzs:
            got("y3", k, dz)
            send(("y2a", k, dz), slot(k, 3, dz, 0), slot(k, 2, dz, 0), yp)
            got("y1", k, dz)
            send(("y2b", k, dz), slot(k, 1, dz, 1), slot(k, 2, dz, 1), ym)

    def y_last(k):
        for dz in range(NZ):
            got("y2a", k, dz)
            got("y2b", k, dz)

    def suffix(k):
        zero = jnp.zeros((ROWS, 128), bf16)
        s = None
        for half in range(2):
            which = core if half == 0 else 1 - core
            cols = pl.ds(pl.multiple_of(which * 256 + k * 128, 128), 128)
            q = qfmt[which, k, 0:ROWS, :]
            q = jnp.concatenate([q, zero] if half == 0 else [zero, q], axis=0)
            keys = sk_in[:, :, cols].reshape(1024, 128)
            more = lax.dot_general(keys, q, NT, preferred_element_type=f32)
            s = more if s is None else s + more
        token = lax.broadcasted_iota(jnp.int32, (1024, 128), 0)
        lane = lax.broadcasted_iota(jnp.int32, (1024, 128), 1)
        branch = lax.broadcasted_iota(jnp.int32, (1, 128), 1) & (OWN - 1)
        length = jnp.zeros((1, 128), jnp.int32)
        for b in range(OWN):
            length = jnp.where(branch == b, len_in[b], length)
        ok = ((token >> 8) == (lane & (OWN - 1))) & ((token & 255) < length)
        top = jnp.max(jnp.where(ok, s, NEG), axis=0, keepdims=True)
        w = jnp.where(ok, jnp.exp2((s - top) * EXP_SCALE), 0.0)
        total = jnp.sum(w, axis=0, keepdims=True)
        w = w.astype(bf16)
        both = []
        for half in range(2):
            which = core if half == 0 else 1 - core
            cols = pl.ds(pl.multiple_of(which * 256 + k * 128, 128), 128)
            values = sv_in[:, :, cols].reshape(1024, 128)
            both.append(lax.dot_general(values, w, TN, preferred_element_type=f32))
        lane = lax.broadcasted_iota(jnp.int32, (128, 128), 1)
        suf_o[k] = jnp.where(lane < ROWS, both[0], both[1])
        suf_ml[k, 0:1] = top
        suf_ml[k, 1:2] = total

    row = lax.broadcasted_iota(jnp.int32, (128, 128), 0)
    lane = lax.broadcasted_iota(jnp.int32, (128, 128), 1)
    block_id = jnp.where(lane < 2, 2 * ctx + lane, 2 * (ctx + 1 - 2 * core) + lane - 2)
    pick = ((row == block_id) & (lane < 4)).astype(f32).astype(bf16)
    row = lax.broadcasted_iota(jnp.int32, (TILE, 256), 0)
    lane = lax.broadcasted_iota(jnp.int32, (TILE, 256), 1)
    spread = ((lane >> 4) == (row >> 6)) & ((lane & 15) == (row & (OWN - 1)))
    spread = spread.astype(f32).astype(bf16)

    def constants():
        row = lax.broadcasted_iota(jnp.int32, (128, 128), 0)
        for j in range(4):
            hide[j] = jnp.where(row == j, NEG, 0.0).astype(bf16)
        row = lax.broadcasted_iota(jnp.int32, (PROWS, 256), 0)
        lane = lax.broadcasted_iota(jnp.int32, (PROWS, 256), 1)
        eye[...] = (row == lane).astype(f32).astype(bf16)

    class Tile:
        def __init__(self, n, k, dys, g):
            self.k, self.dys, self.g = k, dys, g
            self.scores = (scores0, scores1)[n % 2]

        def front(self, j):
            if j == 0:
                slots = slice(4 * self.g, 4 * self.g + 4)
                q = [qbuf[self.k, dy, slots, :, 0:ROWS, :].reshape(TILE // 2, 128) for dy in self.dys]
                q = jnp.concatenate(q, axis=0)
                bits = [qbuf[0, dy, slots, :, ROWS:QROWS, :].reshape(128, 128) for dy in self.dys]
                bits = jnp.concatenate(bits, axis=0)
                unseen = jnp.dot((1.0 - bits.astype(f32)).astype(bf16), pick, preferred_element_type=f32)
                unseen = jnp.dot(spread, unseen.astype(bf16), preferred_element_type=f32)
                self.q = jnp.concatenate([q, unseen.astype(bf16)], axis=1)
                self.top = jnp.full((TILE, 128), NEG, f32)
            keys = jnp.concatenate([kv[self.k, xs, j // 2, 0, j % 2] for xs in range(4)], axis=1)
            keys = jnp.concatenate([keys, jnp.concatenate([hide[j]] * 4, axis=1)], axis=0)
            s = jnp.dot(self.q, keys, preferred_element_type=f32)
            self.scores[:, pl.ds(j * 512, 512)] = s
            for c in range(0, 512, 128):
                self.top = jnp.maximum(self.top, s[:, c : c + 128])

        def back(self, j):
            if j == 0:
                top = jnp.max(self.top, axis=1, keepdims=True)
                self.top = jnp.maximum(top, 0.1 * NEG).astype(bf16).astype(f32)
                self.acc = jnp.zeros((TILE, 256), f32)
            values = jnp.concatenate([kv[self.k, xs, j // 2, 1, j % 2] for xs in range(4)], axis=0)
            values = jnp.concatenate([values, jnp.ones((512, 128), bf16)], axis=1)
            w = jnp.exp2((self.scores[:, pl.ds(j * 512, 512)] - self.top) * EXP_SCALE).astype(bf16)
            self.acc = self.acc + jnp.dot(w, values, preferred_element_type=f32)

        def store(self):
            total = self.acc[:, 128:]
            high = total.astype(bf16).astype(f32)
            lane = lax.broadcasted_iota(jnp.int32, (TILE, 128), 1)
            tail = jnp.where(lane == 0, self.top, jnp.where(lane == 1, high, jnp.where(lane == 2, total - high, 0.0)))
            packed = jnp.concatenate([self.acc[:, :128].astype(bf16), tail.astype(bf16)], axis=1)
            turned = lax.dot_general(eye[...], packed, NT, preferred_element_type=f32).astype(bf16)
            for i in range(8):
                part[self.k, self.dys[i // 4], 4 * self.g + i % 4] = turned[:, i * 128 : i * 128 + 128]

    def fold(pieces):
        total = pieces[0].astype(f32)
        row = lax.broadcasted_iota(jnp.int32, (16, 128), 0)
        for other in pieces[1:-1]:
            values, top, mass = combine(total, other.astype(f32))
            tail = jnp.where(row == 0, top, jnp.where(row == 1, mass, 0.0))
            total = jnp.concatenate([values, tail], axis=0)
        return combine(total, pieces[-1].astype(f32))

    def merge(k, dy, dz, *others):
        dz = place(dz)
        others = [buf[tuple(index)] for buf, *index in others]
        part[k, dy, dz] = pack(*fold([part[k, dy, dz]] + others))

    def y_reduce(k, g, step):
        dzs = [(4 * g + i - 1) % NZ for i in range(4)]
        a, b = pl.ds(4 * g, 2), pl.ds(4 * g + 2, 2)
        if step == 0:
            send(("ra", k, g), part.at[k, 2, a], ra.at[k, g], yp)
            send(("rb", k, g), part.at[k, 2, b], rb.at[k, g], ym)
            send(("rcb", k, g), part.at[k, 1, b], rc.at[k, 0, b], yp)
        elif step == 1:
            send(("rda", k, g), part.at[k, 3, a], rc.at[k, 1, a], ym)
            got("ra", k, g)
            for i in range(2):
                merge(k, 1, dzs[i], (ra, k, g, i))
            send(("rca", k, g), part.at[k, 1, a], rc.at[k, 0, a], yp)
            got("rb", k, g)
            for i in range(2):
                merge(k, 3, dzs[2 + i], (rb, k, g, i))
            send(("rdb", k, g), part.at[k, 3, b], rc.at[k, 1, b], ym)
        else:
            for name in ("rcb", "rda", "rca", "rdb"):
                got(name, k, g)
            for i in (1, 2, 0, 3) if g else (3, 0, 2, 1):
                merge(k, 0, dzs[i], (rc, k, 0, 4 * g + i), (rc, k, 1, 4 * g + i))

    def z_out(k, g):
        for dz in [(4 * g + i - 1) % NZ for i in range(4)]:
            for half in range(2):
                if dz or half:
                    send(("fin", k, half, dz), part.at[k, 0, place(dz)], fin.at[k, half, dz], along_z[half][dz])

    def finish(k):
        lane = lax.broadcasted_iota(jnp.int32, (PROWS, 128), 1)
        pieces = []
        for dz in range(NZ):
            for half in range(2):
                if dz or half:
                    got("fin", k, half, dz)
            first = fin[k, 0, dz] if dz else part[k, 0, place(0)]
            pieces.append(jnp.where(lane < ROWS, first.astype(f32), fin[k, 1, dz].astype(f32)))
        values, top_a, mass = fold(pieces)
        top_b = suf_ml[k, 0:1]
        top = jnp.maximum(top_a, top_b)
        fa = jnp.exp2((top_a - top) * EXP_SCALE)
        fb = jnp.exp2((top_b - top) * EXP_SCALE)
        total = mass * fa + suf_ml[k, 1:2] * fb
        work[...] = ((values * fa + suf_o[k] * fb) / total).T
        for half in range(2):
            which = core if half == 0 else 1 - core
            for h in range(RATIO):
                col = pl.multiple_of((which * 2 + k) * RATIO * HEAD_DIM + h * HEAD_DIM, 128)
                rows = work[pl.ds(half * ROWS + h * OWN, OWN), :]
                out_ref[:, pl.ds(col, HEAD_DIM)] = rows.astype(bf16)

    kv_send(0)
    q_send(0)
    own_kv(1)
    y_send(0, 0)
    queries(1)
    y_send(0, 1, 7, 2, 6)
    kv_forward(0)
    y_send(0, 3, 5, 4)
    kv_send(1)
    q_send(1)
    constants()
    y_forward(0, 0, 1, 7)
    loads[4].wait()
    loads[5].wait()
    suffix(0)
    y_forward(0, 2, 6, 3, 5, 4)
    kv_last(0)

    order = [(0, dys, g) for dys in ((0, 1), (3, 2)) for g in (0, 1)]
    order += [(1, dys, g) for g in (1, 0) for dys in ((2, 1), (3, 0))]
    events = {}

    def at(n, f, *args):
        events.setdefault(n, []).append((f, args))

    at(0, y_send, 1, 0, 1, 7)
    at(1, y_send, 1, 2, 6)
    at(1, kv_forward, 1)
    at(2, y_send, 1, 3, 5, 4)
    at(3, y_last, 0)
    at(5, y_forward, 1, 0, 1, 7, 2)
    at(7, y_forward, 1, 6, 3, 5, 4)
    at(11, kv_last, 1)
    at(11, y_last, 1)
    at(11, y_reduce, 0, 0, 0)
    at(15, y_reduce, 0, 0, 1)
    at(15, y_reduce, 0, 1, 0)
    at(18, y_reduce, 0, 0, 2)
    at(18, z_out, 0, 0)
    at(18, y_reduce, 0, 1, 1)
    at(22, y_reduce, 0, 1, 2)
    at(22, z_out, 0, 1)
    at(19, y_reduce, 1, 1, 0)
    at(23, y_reduce, 1, 1, 1)
    at(26, y_reduce, 1, 1, 2)
    at(26, z_out, 1, 1)
    at(27, y_reduce, 1, 0, 0)
    at(31, y_reduce, 1, 0, 1)
    at(31, suffix, 1)
    at(31, y_reduce, 1, 0, 2)
    at(31, z_out, 1, 0)
    at(31, finish, 0)
    at(31, finish, 1)

    tile = Tile(0, *order[0])
    for j in range(4):
        tile.front(j)
    for n in range(len(order)):
        following = Tile(n + 1, *order[n + 1]) if n + 1 < len(order) else None
        for j in range(4):
            if following is not None:
                following.front(j)
            tile.back(j)
            if j == 3:
                tile.store()
                tile = following
            for f, args in events.get(4 * n + j, []):
                f(*args)
    for name in copies:
        if name not in done:
            copy_of(name).wait_recv()
        copy_of(name).wait_send()


def shards(
    queries, block_lists, suffix_lengths, prompt_keys, prompt_values, suffix_keys, suffix_values
):
    hbm = pl.BlockSpec(memory_space=pltpu.HBM)
    vmem = pl.BlockSpec(memory_space=pltpu.VMEM)
    smem = pl.BlockSpec(memory_space=pltpu.SMEM)
    return pl.pallas_call(
        kernel,
        out_shape=jax.ShapeDtypeStruct(queries.shape, bf16),
        in_specs=[hbm, hbm, smem, hbm, hbm, hbm, hbm],
        out_specs=vmem,
        scratch_shapes=[
            pltpu.VMEM(queries.shape, bf16),
            pltpu.VMEM(block_lists.shape, jnp.int32),
            pltpu.VMEM(prompt_keys.shape, bf16),
            pltpu.VMEM(prompt_values.shape, bf16),
            pltpu.VMEM(suffix_keys.shape, bf16),
            pltpu.VMEM(suffix_values.shape, bf16),
            pltpu.VMEM((2, 2, QROWS, 128), bf16),
            pltpu.VMEM((128, 128), f32),
            pltpu.VMEM((2, NY, NZ, 2, QROWS, 128), bf16),
            pltpu.VMEM((2, 4, 2, 2, 2, 128, 128), bf16),
            pltpu.VMEM((2, 2, 2, 128, 128), bf16),
            pltpu.VMEM((TILE, 2048), f32),
            pltpu.VMEM((TILE, 2048), f32),
            pltpu.VMEM((4, 128, 128), bf16),
            pltpu.VMEM((PROWS, 256), bf16),
            pltpu.VMEM((2, NY, NZ, PROWS, 128), bf16),
            pltpu.VMEM((2, 2, 2, PROWS, 128), bf16),
            pltpu.VMEM((2, 2, 2, PROWS, 128), bf16),
            pltpu.VMEM((2, 2, NZ, PROWS, 128), bf16),
            pltpu.VMEM((2, 2, NZ, PROWS, 128), bf16),
            pltpu.VMEM((2, 128, 128), f32),
            pltpu.VMEM((2, 8, 128), f32),
            pltpu.SemaphoreType.DMA((COPIES,)),
            pltpu.SemaphoreType.DMA((COPIES,)),
            pltpu.SemaphoreType.DMA((6,)),
        ],
        compiler_params=pltpu.CompilerParams(
            collective_id=0, has_side_effects=True, vmem_limit_bytes=56 * 1024 * 1024
        ),
    )(queries, block_lists, suffix_lengths, prompt_keys, prompt_values, suffix_keys, suffix_values)


def solution(mesh):
    return jax.shard_map(
        shards,
        mesh=mesh,
        in_specs=(
            P(("ctx", "slab"), None),
            P(("ctx", "slab"), None),
            P(("ctx", "slab")),
            P("ctx", "slab", None),
            P("ctx", "slab", None),
            P(("ctx", "slab"), None, None),
            P(("ctx", "slab"), None, None),
        ),
        out_specs=P(("ctx", "slab"), None),
        check_vma=False,
    )
```

```python
import jax
import jax.numpy as jnp
from jax import lax
from jax.experimental import pallas as pl
from jax.experimental.pallas import tpu as pltpu
from jax.sharding import PartitionSpec as P

HEADS = 64
KV_HEADS = 4
HEAD_DIM = 128
RATIO = HEADS // KV_HEADS
NEG = -1e30
EXP_SCALE = 1.4426950408889634 / HEAD_DIM**0.5

NX, NY, NZ = 4, 4, 8
OWN = 4
ROWS = 64
QROWS = 80
PROWS = 144
TILE = 1024
COPIES = 192


def place(dz):
    return (dz + 1) % NZ


NT = (((1,), (1,)), ((), ()))
TN = (((0,), (0,)), ((), ()))
f32 = jnp.float32
bf16 = jnp.bfloat16


def combine(a, b):
    top_a, top_b = a[128:129], b[128:129]
    top = jnp.maximum(top_a, top_b)
    fa = jnp.exp2((top_a - top) * EXP_SCALE)
    fb = jnp.exp2((top_b - top) * EXP_SCALE)
    values = a[:128] * fa + b[:128] * fb
    total = (a[129:130] + a[130:131]) * fa + (b[129:130] + b[130:131]) * fb
    return values, top, total


def pack(values, top, total):
    high = total.astype(bf16).astype(f32)
    row = lax.broadcasted_iota(jnp.int32, (16, values.shape[1]), 0)
    tail = jnp.where(row == 0, top, jnp.where(row == 1, high, jnp.where(row == 2, total - high, 0.0)))
    return jnp.concatenate([values.astype(bf16), tail.astype(bf16)], axis=0)


def kernel(
    q_hbm, list_hbm, len_in, k_hbm, v_hbm, sk_hbm, sv_hbm, out_ref,
    q_in, list_in, k_in, v_in, sk_in, sv_in, qfmt, work,
    qbuf, kv, vsib, scores0, scores1, hide, eye, part, ra, rb, rc, fin, suf_o, suf_ml,
    send_sems, recv_sems, loc_sems,
):
    ctx = lax.axis_index("ctx")
    slab = lax.axis_index("slab")
    core = lax.rem(ctx, 2)
    z = lax.rem(ctx // 2, NZ)
    x = slab // 2
    y = lax.rem(slab, 2) * 2 + ctx // (2 * NZ)

    def device(x, y, z, core):
        return (lax.rem(y, 2) * NZ + z) * 2 + core, x * 2 + y // 2

    sib = device(x, y, z, 1 - core)
    xps = [device(lax.rem(x + 1, NX), y, z, c) for c in (core, 1 - core)]
    xms = [device(lax.rem(x + NX - 1, NX), y, z, c) for c in (core, 1 - core)]
    yp = device(x, lax.rem(y + 1, NY), z, core)
    ym = device(x, lax.rem(y + NY - 1, NY), z, core)
    along_z = [[device(x, y, lax.rem(z + dz, NZ), c) for dz in range(NZ)] for c in (core, 1 - core)]

    loads = []
    pairs = ((k_hbm, k_in), (v_hbm, v_in), (q_hbm, q_in), (list_hbm, list_in), (sk_hbm, sk_in), (sv_hbm, sv_in))
    for n, (src, dst) in enumerate(pairs):
        loads.append(pltpu.make_async_copy(src, dst, loc_sems.at[n]))
        loads[n].start()

    barrier = pltpu.get_barrier_semaphore()
    peers = [sib, *xps, *xms, yp, ym] + along_z[0][1:] + along_z[1][1:]
    for other in peers:
        pl.semaphore_signal(barrier, inc=1, device_id=other, device_id_type=pl.DeviceIdType.MESH)

    def own_kv(k):
        mine = pl.ds(pl.multiple_of(core * 256 + k * 128, 128), 128)
        theirs = pl.ds(pl.multiple_of((1 - core) * 256 + k * 128, 128), 128)
        for blk in range(2):
            vsib[k, 0, blk] = k_in[blk, :, theirs].T
            vsib[k, 1, blk] = v_in[blk, :, theirs]
            kv[k, 0, 0, 0, blk] = k_in[blk, :, mine].T
            kv[k, 0, 0, 1, blk] = v_in[blk, :, mine]

    loads[0].wait()
    loads[1].wait()
    own_kv(0)

    loads[2].wait()

    def queries(k):
        for half in range(2):
            for h in range(RATIO):
                col = ((half * 2 + k) * RATIO + h) * HEAD_DIM
                work[pl.ds(h * OWN, OWN), :] = q_in[:, col : col + HEAD_DIM].astype(f32)
            qfmt[half, k, 0:ROWS, :] = work[0:ROWS, :].astype(bf16)

    queries(0)
    loads[3].wait()
    lists = list_in[...]
    lane = lax.broadcasted_iota(jnp.int32, (OWN, 128), 1)
    seen = jnp.zeros((OWN, 128), f32)
    for n in range(lists.shape[1]):
        seen = jnp.where(lists[:, n : n + 1] == lane, 1.0, seen)
    work[0:16, :] = jnp.zeros((16, 128), f32)
    work[0:OWN, :] = seen
    for half in range(2):
        qfmt[half, 0, ROWS:QROWS, :] = work[0:16, :].astype(bf16)

    pl.semaphore_wait(barrier, len(peers))

    copies = {}
    done = set()

    def copy_of(name):
        n, src, dst, to = copies[name]
        return pltpu.make_async_remote_copy(
            src_ref=src, dst_ref=dst, send_sem=send_sems.at[n], recv_sem=recv_sems.at[n],
            device_id=to, device_id_type=pl.DeviceIdType.MESH,
        )

    def send(name, src, dst, to):
        copies[name] = (len(copies), src, dst, to)
        copy_of(name).start()

    def got(*name):
        if name not in done:
            done.add(name)
            copy_of(name).wait_recv()

    def kv_send(k):
        send(("kvsib", k), vsib.at[k], kv.at[k, 0, 1], sib)
        for c, src in enumerate((kv.at[k, 0, 0], vsib.at[k])):
            send(("kv1", k, c), src, kv.at[k, 1, c], xps[c])
            send(("kv2", k, c), src, kv.at[k, 2, c], xms[c])

    def kv_forward(k):
        got("kv1", k, 0)
        send(("kv3", k, 0), kv.at[k, 1, 0], kv.at[k, 3, 0], xps[0])
        got("kv2", k, 1)
        send(("kv3", k, 1), kv.at[k, 2, 1], kv.at[k, 3, 1], xms[0])

    def kv_last(k):
        got("kvsib", k)
        for c in range(2):
            for name in ("kv1", "kv2", "kv3"):
                got(name, k, c)

    def slot(k, dy, dz, which):
        rows = pl.ds(0, QROWS if k == 0 else ROWS)
        if which == 2:
            return qbuf.at[k, dy, place(dz), pl.ds(0, 2), rows]
        return qbuf.at[k, dy, place(dz), which, rows]

    def q_send(k):
        end = QROWS if k == 0 else ROWS
        qbuf[k, 0, place(0), 0, 0:end, :] = qfmt[core, k, 0:end, :]
        for to in (0, 1, 7, 2, 6, 3, 5, 4):
            for half in range(2):
                if to or half:
                    src = qfmt.at[core if half == 0 else 1 - core, k, pl.ds(0, end)]
                    send(("q", k, half, -to % NZ), src, slot(k, 0, -to, half), along_z[half][to])

    def group(k, dy, g, which):
        rows = pl.ds(0, QROWS if k == 0 else ROWS)
        if which == 2:
            return qbuf.at[k, dy, pl.ds(4 * g, 4), pl.ds(0, 2), rows]
        return qbuf.at[k, dy, pl.ds(4 * g, 4), which, rows]

    def y_send(k, g):
        for dz in ((0, 1, 7, 2), (6, 3, 5, 4))[g]:
            for half in range(2):
                if dz or half:
                    got("q", k, half, dz)
        send(("y3", k, g), group(k, 0, g, 2), group(k, 3, g, 2), yp)
        send(("y1", k, g), group(k, 0, g, 2), group(k, 1, g, 2), ym)

    def y_forward(k, g):
        got("y3", k, g)
        send(("y2a", k, g), group(k, 3, g, 0), group(k, 2, g, 0), yp)
        got("y1", k, g)
        send(("y2b", k, g), group(k, 1, g, 1), group(k, 2, g, 1), ym)

    def y_last(k):
        for g in range(2):
            got("y2a", k, g)
            got("y2b", k, g)

    def suffix(k):
        zero = jnp.zeros((ROWS, 128), bf16)
        s = None
        for half in range(2):
            which = core if half == 0 else 1 - core
            cols = pl.ds(pl.multiple_of(which * 256 + k * 128, 128), 128)
            q = qfmt[which, k, 0:ROWS, :]
            q = jnp.concatenate([q, zero] if half == 0 else [zero, q], axis=0)
            keys = sk_in[:, :, cols].reshape(1024, 128)
            more = lax.dot_general(keys, q, NT, preferred_element_type=f32)
            s = more if s is None else s + more
        token = lax.broadcasted_iota(jnp.int32, (1024, 128), 0)
        lane = lax.broadcasted_iota(jnp.int32, (1024, 128), 1)
        branch = lax.broadcasted_iota(jnp.int32, (1, 128), 1) & (OWN - 1)
        length = jnp.zeros((1, 128), jnp.int32)
        for b in range(OWN):
            length = jnp.where(branch == b, len_in[b], length)
        ok = ((token >> 8) == (lane & (OWN - 1))) & ((token & 255) < length)
        top = jnp.max(jnp.where(ok, s, NEG), axis=0, keepdims=True)
        w = jnp.where(ok, jnp.exp2((s - top) * EXP_SCALE), 0.0)
        total = jnp.sum(w, axis=0, keepdims=True)
        w = w.astype(bf16)
        both = []
        for half in range(2):
            which = core if half == 0 else 1 - core
            cols = pl.ds(pl.multiple_of(which * 256 + k * 128, 128), 128)
            values = sv_in[:, :, cols].reshape(1024, 128)
            both.append(lax.dot_general(values, w, TN, preferred_element_type=f32))
        lane = lax.broadcasted_iota(jnp.int32, (128, 128), 1)
        suf_o[k] = jnp.where(lane < ROWS, both[0], both[1])
        suf_ml[k, 0:1] = top
        suf_ml[k, 1:2] = total

    row = lax.broadcasted_iota(jnp.int32, (128, 128), 0)
    lane = lax.broadcasted_iota(jnp.int32, (128, 128), 1)
    block_id = jnp.where(lane < 2, 2 * ctx + lane, 2 * (ctx + 1 - 2 * core) + lane - 2)
    pick = ((row == block_id) & (lane < 4)).astype(f32).astype(bf16)
    row = lax.broadcasted_iota(jnp.int32, (TILE, 256), 0)
    lane = lax.broadcasted_iota(jnp.int32, (TILE, 256), 1)
    spread = ((lane >> 4) == (row >> 6)) & ((lane & 15) == (row & (OWN - 1)))
    spread = spread.astype(f32).astype(bf16)

    def constants():
        row = lax.broadcasted_iota(jnp.int32, (128, 128), 0)
        for j in range(4):
            hide[j] = jnp.where(row == j, NEG, 0.0).astype(bf16)
        row = lax.broadcasted_iota(jnp.int32, (PROWS, 256), 0)
        lane = lax.broadcasted_iota(jnp.int32, (PROWS, 256), 1)
        eye[...] = (row == lane).astype(f32).astype(bf16)

    class Tile:
        def __init__(self, n, k, dys, g):
            self.k, self.dys, self.g = k, dys, g
            self.scores = (scores0, scores1)[n % 2]

        def front(self, j):
            if j == 0:
                slots = slice(4 * self.g, 4 * self.g + 4)
                q = [qbuf[self.k, dy, slots, :, 0:ROWS, :].reshape(TILE // 2, 128) for dy in self.dys]
                q = jnp.concatenate(q, axis=0)
                bits = [qbuf[0, dy, slots, :, ROWS:QROWS, :].reshape(128, 128) for dy in self.dys]
                bits = jnp.concatenate(bits, axis=0)
                unseen = jnp.dot((1.0 - bits.astype(f32)).astype(bf16), pick, preferred_element_type=f32)
                unseen = jnp.dot(spread, unseen.astype(bf16), preferred_element_type=f32)
                self.q = jnp.concatenate([q, unseen.astype(bf16)], axis=1)
                self.top = jnp.full((TILE, 128), NEG, f32)
            keys = jnp.concatenate([kv[self.k, xs, j // 2, 0, j % 2] for xs in range(4)], axis=1)
            keys = jnp.concatenate([keys, jnp.concatenate([hide[j]] * 4, axis=1)], axis=0)
            s = jnp.dot(self.q, keys, preferred_element_type=f32)
            self.scores[:, pl.ds(j * 512, 512)] = s
            for c in range(0, 512, 128):
                self.top = jnp.maximum(self.top, s[:, c : c + 128])

        def back(self, j):
            if j == 0:
                top = jnp.max(self.top, axis=1, keepdims=True)
                self.top = jnp.maximum(top, 0.1 * NEG).astype(bf16).astype(f32)
                self.acc = jnp.zeros((TILE, 256), f32)
            values = jnp.concatenate([kv[self.k, xs, j // 2, 1, j % 2] for xs in range(4)], axis=0)
            values = jnp.concatenate([values, jnp.ones((512, 128), bf16)], axis=1)
            w = jnp.exp2((self.scores[:, pl.ds(j * 512, 512)] - self.top) * EXP_SCALE).astype(bf16)
            self.acc = self.acc + jnp.dot(w, values, preferred_element_type=f32)

        def store(self):
            total = self.acc[:, 128:]
            high = total.astype(bf16).astype(f32)
            lane = lax.broadcasted_iota(jnp.int32, (TILE, 128), 1)
            tail = jnp.where(lane == 0, self.top, jnp.where(lane == 1, high, jnp.where(lane == 2, total - high, 0.0)))
            packed = jnp.concatenate([self.acc[:, :128].astype(bf16), tail.astype(bf16)], axis=1)
            turned = lax.dot_general(eye[...], packed, NT, preferred_element_type=f32).astype(bf16)
            for i in range(8):
                part[self.k, self.dys[i // 4], 4 * self.g + i % 4] = turned[:, i * 128 : i * 128 + 128]

    def fold(pieces):
        total = pieces[0].astype(f32)
        row = lax.broadcasted_iota(jnp.int32, (16, 128), 0)
        for other in pieces[1:-1]:
            values, top, mass = combine(total, other.astype(f32))
            tail = jnp.where(row == 0, top, jnp.where(row == 1, mass, 0.0))
            total = jnp.concatenate([values, tail], axis=0)
        return combine(total, pieces[-1].astype(f32))

    def merge(k, dy, dz, *others):
        dz = place(dz)
        others = [buf[tuple(index)] for buf, *index in others]
        part[k, dy, dz] = pack(*fold([part[k, dy, dz]] + others))

    def y_reduce(k, g, step):
        dzs = [(4 * g + i - 1) % NZ for i in range(4)]
        a, b = pl.ds(4 * g, 2), pl.ds(4 * g + 2, 2)
        if step == 0:
            send(("ra", k, g), part.at[k, 2, a], ra.at[k, g], yp)
            send(("rb", k, g), part.at[k, 2, b], rb.at[k, g], ym)
            send(("rcb", k, g), part.at[k, 1, b], rc.at[k, 0, b], yp)
        elif step == 1:
            send(("rda", k, g), part.at[k, 3, a], rc.at[k, 1, a], ym)
            got("ra", k, g)
            for i in range(2):
                merge(k, 1, dzs[i], (ra, k, g, i))
            send(("rca", k, g), part.at[k, 1, a], rc.at[k, 0, a], yp)
            got("rb", k, g)
            for i in range(2):
                merge(k, 3, dzs[2 + i], (rb, k, g, i))
            send(("rdb", k, g), part.at[k, 3, b], rc.at[k, 1, b], ym)
        else:
            for name in ("rcb", "rda", "rca", "rdb"):
                got(name, k, g)
            for i in (1, 2, 0, 3) if g else (3, 0, 2, 1):
                merge(k, 0, dzs[i], (rc, k, 0, 4 * g + i), (rc, k, 1, 4 * g + i))

    def z_out(k, g):
        for dz in [(4 * g + i - 1) % NZ for i in range(4)]:
            for half in range(2):
                if dz or half:
                    send(("fin", k, half, dz), part.at[k, 0, place(dz)], fin.at[k, half, dz], along_z[half][dz])

    def finish(k):
        lane = lax.broadcasted_iota(jnp.int32, (PROWS, 128), 1)
        pieces = []
        for dz in range(NZ):
            for half in range(2):
                if dz or half:
                    got("fin", k, half, dz)
            first = fin[k, 0, dz] if dz else part[k, 0, place(0)]
            pieces.append(jnp.where(lane < ROWS, first.astype(f32), fin[k, 1, dz].astype(f32)))
        values, top_a, mass = fold(pieces)
        top_b = suf_ml[k, 0:1]
        top = jnp.maximum(top_a, top_b)
        fa = jnp.exp2((top_a - top) * EXP_SCALE)
        fb = jnp.exp2((top_b - top) * EXP_SCALE)
        total = mass * fa + suf_ml[k, 1:2] * fb
        work[...] = ((values * fa + suf_o[k] * fb) / total).T
        for half in range(2):
            which = core if half == 0 else 1 - core
            for b in range(OWN):
                rows = work[pl.ds(half * ROWS + b, RATIO, stride=OWN), :]
                out_ref[b, which * 2 + k] = rows.astype(bf16)

    kv_send(0)
    q_send(0)
    own_kv(1)
    y_send(0, 0)
    queries(1)
    kv_forward(0)
    y_send(0, 1)
    kv_send(1)
    q_send(1)
    constants()
    y_forward(0, 0)
    loads[4].wait()
    loads[5].wait()
    suffix(0)
    kv_last(0)

    order = [(0, dys, g) for dys in ((0, 1), (3, 2)) for g in (0, 1)]
    order += [(1, dys, g) for g in (1, 0) for dys in ((2, 1), (3, 0))]
    events = {}

    def at(n, f, *args):
        events.setdefault(n, []).append((f, args))

    at(0, y_send, 1, 0)
    at(1, kv_forward, 1)
    at(2, y_send, 1, 1)
    at(3, y_last, 0)
    at(5, y_forward, 1, 0)
    at(7, y_forward, 1, 1)
    at(11, kv_last, 1)
    at(11, y_last, 1)
    at(11, y_reduce, 0, 0, 0)
    at(15, y_reduce, 0, 0, 1)
    at(15, y_reduce, 0, 1, 0)
    at(18, y_reduce, 0, 0, 2)
    at(18, z_out, 0, 0)
    at(18, y_reduce, 0, 1, 1)
    at(22, y_reduce, 0, 1, 2)
    at(22, z_out, 0, 1)
    at(19, y_reduce, 1, 1, 0)
    at(23, y_reduce, 1, 1, 1)
    at(26, y_reduce, 1, 1, 2)
    at(26, z_out, 1, 1)
    at(27, y_reduce, 1, 0, 0)
    at(31, y_reduce, 1, 0, 1)
    at(31, suffix, 1)
    at(31, y_reduce, 1, 0, 2)
    at(31, z_out, 1, 0)
    at(31, finish, 0)
    at(31, finish, 1)

    tile = Tile(0, *order[0])
    for j in range(4):
        tile.front(j)
    y_forward(0, 1)
    for n in range(len(order)):
        following = Tile(n + 1, *order[n + 1]) if n + 1 < len(order) else None
        for j in range(4):
            if following is not None:
                following.front(j)
            tile.back(j)
            if j == 3:
                tile.store()
                tile = following
            for f, args in events.get(4 * n + j, []):
                f(*args)
    for name in copies:
        if name not in done:
            copy_of(name).wait_recv()
        copy_of(name).wait_send()


def shards(
    queries, block_lists, suffix_lengths, prompt_keys, prompt_values, suffix_keys, suffix_values
):
    hbm = pl.BlockSpec(memory_space=pltpu.HBM)
    vmem = pl.BlockSpec(memory_space=pltpu.VMEM)
    smem = pl.BlockSpec(memory_space=pltpu.SMEM)
    out = pl.pallas_call(
        kernel,
        out_shape=jax.ShapeDtypeStruct((OWN, KV_HEADS, RATIO, HEAD_DIM), bf16),
        in_specs=[hbm, hbm, smem, hbm, hbm, hbm, hbm],
        out_specs=vmem,
        scratch_shapes=[
            pltpu.VMEM(queries.shape, bf16),
            pltpu.VMEM(block_lists.shape, jnp.int32),
            pltpu.VMEM(prompt_keys.shape, bf16),
            pltpu.VMEM(prompt_values.shape, bf16),
            pltpu.VMEM(suffix_keys.shape, bf16),
            pltpu.VMEM(suffix_values.shape, bf16),
            pltpu.VMEM((2, 2, QROWS, 128), bf16),
            pltpu.VMEM((128, 128), f32),
            pltpu.VMEM((2, NY, NZ, 2, QROWS, 128), bf16),
            pltpu.VMEM((2, 4, 2, 2, 2, 128, 128), bf16),
            pltpu.VMEM((2, 2, 2, 128, 128), bf16),
            pltpu.VMEM((TILE, 2048), f32),
            pltpu.VMEM((TILE, 2048), f32),
            pltpu.VMEM((4, 128, 128), bf16),
            pltpu.VMEM((PROWS, 256), bf16),
            pltpu.VMEM((2, NY, NZ, PROWS, 128), bf16),
            pltpu.VMEM((2, 2, 2, PROWS, 128), bf16),
            pltpu.VMEM((2, 2, 2, PROWS, 128), bf16),
            pltpu.VMEM((2, 2, NZ, PROWS, 128), bf16),
            pltpu.VMEM((2, 2, NZ, PROWS, 128), bf16),
            pltpu.VMEM((2, 128, 128), f32),
            pltpu.VMEM((2, 8, 128), f32),
            pltpu.SemaphoreType.DMA((COPIES,)),
            pltpu.SemaphoreType.DMA((COPIES,)),
            pltpu.SemaphoreType.DMA((6,)),
        ],
        compiler_params=pltpu.CompilerParams(
            collective_id=0, has_side_effects=True, vmem_limit_bytes=56 * 1024 * 1024
        ),
    )(queries, block_lists, suffix_lengths, prompt_keys, prompt_values, suffix_keys, suffix_values)
    return out.reshape(queries.shape)


def solution(mesh):
    return jax.shard_map(
        shards,
        mesh=mesh,
        in_specs=(
            P(("ctx", "slab"), None),
            P(("ctx", "slab"), None),
            P(("ctx", "slab")),
            P("ctx", "slab", None),
            P("ctx", "slab", None),
            P(("ctx", "slab"), None, None),
            P(("ctx", "slab"), None, None),
        ),
        out_specs=P(("ctx", "slab"), None),
        check_vma=False,
    )
```

```python
import jax
import jax.numpy as jnp
from jax import lax
from jax.experimental import pallas as pl
from jax.experimental.pallas import tpu as pltpu
from jax.sharding import PartitionSpec as P

HEADS = 64
KV_HEADS = 4
HEAD_DIM = 128
RATIO = HEADS // KV_HEADS
NEG = -1e30
EXP_SCALE = 1.4426950408889634 / HEAD_DIM**0.5

NX, NY, NZ = 4, 4, 8
OWN = 4
ROWS = 64
QROWS = 80
PROWS = 144
TILE = 1024
COPIES = 192


def place(dz):
    return (dz + 1) % NZ


NT = (((1,), (1,)), ((), ()))
TN = (((0,), (0,)), ((), ()))
f32 = jnp.float32
bf16 = jnp.bfloat16


def combine(a, b):
    top_a, top_b = a[128:129], b[128:129]
    top = jnp.maximum(top_a, top_b)
    fa = jnp.exp2((top_a - top) * EXP_SCALE)
    fb = jnp.exp2((top_b - top) * EXP_SCALE)
    values = a[:128] * fa + b[:128] * fb
    total = (a[129:130] + a[130:131]) * fa + (b[129:130] + b[130:131]) * fb
    return values, top, total


def pack(values, top, total):
    high = total.astype(bf16).astype(f32)
    row = lax.broadcasted_iota(jnp.int32, (16, values.shape[1]), 0)
    tail = jnp.where(row == 0, top, jnp.where(row == 1, high, jnp.where(row == 2, total - high, 0.0)))
    return jnp.concatenate([values.astype(bf16), tail.astype(bf16)], axis=0)


def kernel(
    q_hbm, list_hbm, len_in, k_hbm, v_hbm, sk_hbm, sv_hbm, out_ref,
    q_in, list_in, k_in, v_in, sk_in, sv_in, qfmt, work,
    qbuf, kv, vsib, scores0, scores1, hide, eye, part, ra, rb, rc, fin, suf_o, suf_ml,
    send_sems, recv_sems, loc_sems,
):
    ctx = lax.axis_index("ctx")
    slab = lax.axis_index("slab")
    core = lax.rem(ctx, 2)
    z = lax.rem(ctx // 2, NZ)
    x = slab // 2
    y = lax.rem(slab, 2) * 2 + ctx // (2 * NZ)

    def device(x, y, z, core):
        return (lax.rem(y, 2) * NZ + z) * 2 + core, x * 2 + y // 2

    sib = device(x, y, z, 1 - core)
    xps = [device(lax.rem(x + 1, NX), y, z, c) for c in (core, 1 - core)]
    xms = [device(lax.rem(x + NX - 1, NX), y, z, c) for c in (core, 1 - core)]
    yp = device(x, lax.rem(y + 1, NY), z, core)
    ym = device(x, lax.rem(y + NY - 1, NY), z, core)
    along_z = [[device(x, y, lax.rem(z + dz, NZ), c) for dz in range(NZ)] for c in (core, 1 - core)]

    loads = []
    pairs = ((k_hbm, k_in), (v_hbm, v_in), (q_hbm, q_in), (list_hbm, list_in), (sk_hbm, sk_in), (sv_hbm, sv_in))
    for n, (src, dst) in enumerate(pairs):
        loads.append(pltpu.make_async_copy(src, dst, loc_sems.at[n]))
        loads[n].start()

    barrier = pltpu.get_barrier_semaphore()
    peers = [sib, *xps, *xms, yp, ym] + along_z[0][1:] + along_z[1][1:]
    for other in peers:
        pl.semaphore_signal(barrier, inc=1, device_id=other, device_id_type=pl.DeviceIdType.MESH)

    def own_kv(k):
        mine = pl.ds(pl.multiple_of(core * 256 + k * 128, 128), 128)
        theirs = pl.ds(pl.multiple_of((1 - core) * 256 + k * 128, 128), 128)
        for blk in range(2):
            vsib[k, 0, blk] = k_in[blk, :, theirs].T
            vsib[k, 1, blk] = v_in[blk, :, theirs]
            kv[k, 0, 0, 0, blk] = k_in[blk, :, mine].T
            kv[k, 0, 0, 1, blk] = v_in[blk, :, mine]

    loads[0].wait()
    loads[1].wait()
    own_kv(0)

    loads[2].wait()

    def queries(k):
        for half in range(2):
            for h in range(RATIO):
                col = ((half * 2 + k) * RATIO + h) * HEAD_DIM
                work[pl.ds(h * OWN, OWN), :] = q_in[:, col : col + HEAD_DIM].astype(f32)
            qfmt[half, k, 0:ROWS, :] = work[0:ROWS, :].astype(bf16)

    queries(0)
    loads[3].wait()
    lists = list_in[...]
    lane = lax.broadcasted_iota(jnp.int32, (OWN, 128), 1)
    seen = jnp.zeros((OWN, 128), f32)
    for n in range(lists.shape[1]):
        seen = jnp.where(lists[:, n : n + 1] == lane, 1.0, seen)
    work[0:16, :] = jnp.zeros((16, 128), f32)
    work[0:OWN, :] = seen
    for half in range(2):
        qfmt[half, 0, ROWS:QROWS, :] = work[0:16, :].astype(bf16)

    pl.semaphore_wait(barrier, len(peers))

    copies = {}
    done = set()

    def copy_of(name):
        n, src, dst, to = copies[name]
        return pltpu.make_async_remote_copy(
            src_ref=src, dst_ref=dst, send_sem=send_sems.at[n], recv_sem=recv_sems.at[n],
            device_id=to, device_id_type=pl.DeviceIdType.MESH,
        )

    def send(name, src, dst, to):
        copies[name] = (len(copies), src, dst, to)
        copy_of(name).start()

    def got(*name):
        if name not in done:
            done.add(name)
            copy_of(name).wait_recv()

    def kv_send(k):
        send(("kvsib", k), vsib.at[k], kv.at[k, 0, 1], sib)
        for c, src in enumerate((kv.at[k, 0, 0], vsib.at[k])):
            send(("kv1", k, c), src, kv.at[k, 1, c], xps[c])
            send(("kv2", k, c), src, kv.at[k, 2, c], xms[c])

    def kv_forward(k):
        got("kv1", k, 0)
        send(("kv3", k, 0), kv.at[k, 1, 0], kv.at[k, 3, 0], xps[0])
        got("kv2", k, 1)
        send(("kv3", k, 1), kv.at[k, 2, 1], kv.at[k, 3, 1], xms[0])

    def kv_last(k):
        got("kvsib", k)
        for c in range(2):
            for name in ("kv1", "kv2", "kv3"):
                got(name, k, c)

    def slot(k, dy, dz, which):
        rows = pl.ds(0, QROWS if k == 0 else ROWS)
        if which == 2:
            return qbuf.at[k, dy, place(dz), pl.ds(0, 2), rows]
        return qbuf.at[k, dy, place(dz), which, rows]

    def q_send(k):
        end = QROWS if k == 0 else ROWS
        qbuf[k, 0, place(0), 0, 0:end, :] = qfmt[core, k, 0:end, :]
        for to in (0, 1, 7, 2, 6, 3, 5, 4):
            for half in range(2):
                if to or half:
                    src = qfmt.at[core if half == 0 else 1 - core, k, pl.ds(0, end)]
                    send(("q", k, half, -to % NZ), src, slot(k, 0, -to, half), along_z[half][to])

    def y_send(k, *dzs):
        for dz in dzs:
            for half in range(2):
                if dz or half:
                    got("q", k, half, dz)
            send(("y3", k, dz), slot(k, 0, dz, 2), slot(k, 3, dz, 2), yp)
            send(("y1", k, dz), slot(k, 0, dz, 2), slot(k, 1, dz, 2), ym)

    def y_forward(k, *dzs):
        for dz in dzs:
            got("y3", k, dz)
            send(("y2a", k, dz), slot(k, 3, dz, 0), slot(k, 2, dz, 0), yp)
            got("y1", k, dz)
            send(("y2b", k, dz), slot(k, 1, dz, 1), slot(k, 2, dz, 1), ym)

    def y_last(k):
        for dz in range(NZ):
            got("y2a", k, dz)
            got("y2b", k, dz)

    def suffix(k):
        zero = jnp.zeros((ROWS, 128), bf16)
        s = None
        for half in range(2):
            which = core if half == 0 else 1 - core
            cols = pl.ds(pl.multiple_of(which * 256 + k * 128, 128), 128)
            q = qfmt[which, k, 0:ROWS, :]
            q = jnp.concatenate([q, zero] if half == 0 else [zero, q], axis=0)
            keys = sk_in[:, :, cols].reshape(1024, 128)
            more = lax.dot_general(keys, q, NT, preferred_element_type=f32)
            s = more if s is None else s + more
        token = lax.broadcasted_iota(jnp.int32, (1024, 128), 0)
        lane = lax.broadcasted_iota(jnp.int32, (1024, 128), 1)
        branch = lax.broadcasted_iota(jnp.int32, (1, 128), 1) & (OWN - 1)
        length = jnp.zeros((1, 128), jnp.int32)
        for b in range(OWN):
            length = jnp.where(branch == b, len_in[b], length)
        ok = ((token >> 8) == (lane & (OWN - 1))) & ((token & 255) < length)
        top = jnp.max(jnp.where(ok, s, NEG), axis=0, keepdims=True)
        w = jnp.where(ok, jnp.exp2((s - top) * EXP_SCALE), 0.0)
        total = jnp.sum(w, axis=0, keepdims=True)
        w = w.astype(bf16)
        both = []
        for half in range(2):
            which = core if half == 0 else 1 - core
            cols = pl.ds(pl.multiple_of(which * 256 + k * 128, 128), 128)
            values = sv_in[:, :, cols].reshape(1024, 128)
            both.append(lax.dot_general(values, w, TN, preferred_element_type=f32))
        lane = lax.broadcasted_iota(jnp.int32, (128, 128), 1)
        suf_o[k] = jnp.where(lane < ROWS, both[0], both[1])
        suf_ml[k, 0:1] = top
        suf_ml[k, 1:2] = total

    row = lax.broadcasted_iota(jnp.int32, (128, 128), 0)
    lane = lax.broadcasted_iota(jnp.int32, (128, 128), 1)
    block_id = jnp.where(lane < 2, 2 * ctx + lane, 2 * (ctx + 1 - 2 * core) + lane - 2)
    pick = ((row == block_id) & (lane < 4)).astype(f32).astype(bf16)
    row = lax.broadcasted_iota(jnp.int32, (TILE, 256), 0)
    lane = lax.broadcasted_iota(jnp.int32, (TILE, 256), 1)
    spread = ((lane >> 4) == (row >> 6)) & ((lane & 15) == (row & (OWN - 1)))
    spread = spread.astype(f32).astype(bf16)

    def constants():
        row = lax.broadcasted_iota(jnp.int32, (128, 128), 0)
        for j in range(4):
            hide[j] = jnp.where(row == j, NEG, 0.0).astype(bf16)
        row = lax.broadcasted_iota(jnp.int32, (PROWS, 256), 0)
        lane = lax.broadcasted_iota(jnp.int32, (PROWS, 256), 1)
        eye[...] = (row == lane).astype(f32).astype(bf16)

    class Tile:
        def __init__(self, n, k, dys, g):
            self.k, self.dys, self.g = k, dys, g
            self.scores = (scores0, scores1)[n % 2]

        def front(self, j):
            if j == 0:
                slots = slice(4 * self.g, 4 * self.g + 4)
                q = [qbuf[self.k, dy, slots, :, 0:ROWS, :].reshape(TILE // 2, 128) for dy in self.dys]
                q = jnp.concatenate(q, axis=0)
                bits = [qbuf[0, dy, slots, :, ROWS:QROWS, :].reshape(128, 128) for dy in self.dys]
                bits = jnp.concatenate(bits, axis=0)
                unseen = jnp.dot((1.0 - bits.astype(f32)).astype(bf16), pick, preferred_element_type=f32)
                unseen = jnp.dot(spread, unseen.astype(bf16), preferred_element_type=f32)
                self.q = jnp.concatenate([q, unseen.astype(bf16)], axis=1)
                self.top = jnp.full((TILE, 128), NEG, f32)
            keys = jnp.concatenate([kv[self.k, xs, j // 2, 0, j % 2] for xs in range(4)], axis=1)
            keys = jnp.concatenate([keys, jnp.concatenate([hide[j]] * 4, axis=1)], axis=0)
            s = jnp.dot(self.q, keys, preferred_element_type=f32)
            self.scores[:, pl.ds(j * 512, 512)] = s
            for c in range(0, 512, 128):
                self.top = jnp.maximum(self.top, s[:, c : c + 128])

        def back(self, j):
            if j == 0:
                top = jnp.max(self.top, axis=1, keepdims=True)
                self.top = jnp.maximum(top, 0.1 * NEG).astype(bf16).astype(f32)
                self.acc = jnp.zeros((TILE, 256), f32)
            values = jnp.concatenate([kv[self.k, xs, j // 2, 1, j % 2] for xs in range(4)], axis=0)
            values = jnp.concatenate([values, jnp.ones((512, 128), bf16)], axis=1)
            w = jnp.exp2((self.scores[:, pl.ds(j * 512, 512)] - self.top) * EXP_SCALE).astype(bf16)
            self.acc = self.acc + jnp.dot(w, values, preferred_element_type=f32)

        def store(self):
            total = self.acc[:, 128:]
            high = total.astype(bf16).astype(f32)
            lane = lax.broadcasted_iota(jnp.int32, (TILE, 128), 1)
            tail = jnp.where(lane == 0, self.top, jnp.where(lane == 1, high, jnp.where(lane == 2, total - high, 0.0)))
            packed = jnp.concatenate([self.acc[:, :128].astype(bf16), tail.astype(bf16)], axis=1)
            turned = lax.dot_general(eye[...], packed, NT, preferred_element_type=f32).astype(bf16)
            for i in range(8):
                part[self.k, self.dys[i // 4], 4 * self.g + i % 4] = turned[:, i * 128 : i * 128 + 128]

    def fold(pieces):
        total = pieces[0].astype(f32)
        row = lax.broadcasted_iota(jnp.int32, (16, 128), 0)
        for other in pieces[1:-1]:
            values, top, mass = combine(total, other.astype(f32))
            tail = jnp.where(row == 0, top, jnp.where(row == 1, mass, 0.0))
            total = jnp.concatenate([values, tail], axis=0)
        return combine(total, pieces[-1].astype(f32))

    def merge(k, dy, dz, *others):
        dz = place(dz)
        others = [buf[tuple(index)] for buf, *index in others]
        part[k, dy, dz] = pack(*fold([part[k, dy, dz]] + others))

    def y_reduce(k, g, step):
        dzs = [(4 * g + i - 1) % NZ for i in range(4)]
        a, b = pl.ds(4 * g, 2), pl.ds(4 * g + 2, 2)
        if step == 0:
            send(("ra", k, g), part.at[k, 2, a], ra.at[k, g], yp)
            send(("rb", k, g), part.at[k, 2, b], rb.at[k, g], ym)
            send(("rcb", k, g), part.at[k, 1, b], rc.at[k, 0, b], yp)
        elif step == 1:
            send(("rda", k, g), part.at[k, 3, a], rc.at[k, 1, a], ym)
            got("ra", k, g)
            for i in range(2):
                merge(k, 1, dzs[i], (ra, k, g, i))
            send(("rca", k, g), part.at[k, 1, a], rc.at[k, 0, a], yp)
            got("rb", k, g)
            for i in range(2):
                merge(k, 3, dzs[2 + i], (rb, k, g, i))
            send(("rdb", k, g), part.at[k, 3, b], rc.at[k, 1, b], ym)
        else:
            for name in ("rcb", "rda", "rca", "rdb"):
                got(name, k, g)
            for i in (1, 2, 0, 3) if g else (3, 0, 2, 1):
                merge(k, 0, dzs[i], (rc, k, 0, 4 * g + i), (rc, k, 1, 4 * g + i))

    def z_out(k, g):
        for dz in [(4 * g + i - 1) % NZ for i in range(4)]:
            for half in range(2):
                if dz or half:
                    send(("fin", k, half, dz), part.at[k, 0, place(dz)], fin.at[k, half, dz], along_z[half][dz])

    def finish(k):
        lane = lax.broadcasted_iota(jnp.int32, (PROWS, 128), 1)
        pieces = []
        for dz in range(NZ):
            for half in range(2):
                if dz or half:
                    got("fin", k, half, dz)
            first = fin[k, 0, dz] if dz else part[k, 0, place(0)]
            pieces.append(jnp.where(lane < ROWS, first.astype(f32), fin[k, 1, dz].astype(f32)))
        values, top_a, mass = fold(pieces)
        top_b = suf_ml[k, 0:1]
        top = jnp.maximum(top_a, top_b)
        fa = jnp.exp2((top_a - top) * EXP_SCALE)
        fb = jnp.exp2((top_b - top) * EXP_SCALE)
        total = mass * fa + suf_ml[k, 1:2] * fb
        work[...] = ((values * fa + suf_o[k] * fb) / total).T
        for half in range(2):
            which = core if half == 0 else 1 - core
            for h in range(RATIO):
                col = pl.multiple_of((which * 2 + k) * RATIO * HEAD_DIM + h * HEAD_DIM, 128)
                rows = work[pl.ds(half * ROWS + h * OWN, OWN), :]
                out_ref[:, pl.ds(col, HEAD_DIM)] = rows.astype(bf16)

    kv_send(0)
    q_send(0)
    own_kv(1)
    y_send(0, 0, 1, 7, 2, 6)
    kv_forward(0)
    y_send(0, 3, 5, 4)
    y_forward(0, 0, 1, 7)
    queries(1)
    kv_send(1)
    q_send(1)
    constants()
    y_forward(0, 2, 6)
    loads[4].wait()
    loads[5].wait()
    suffix(0)
    kv_last(0)

    order = [(0, dys, g) for dys in ((0, 1), (3, 2)) for g in (0, 1)]
    order += [(1, dys, g) for g in (1, 0) for dys in ((2, 1), (3, 0))]
    events = {}

    def at(n, f, *args):
        events.setdefault(n, []).append((f, args))

    at(0, y_send, 1, 0, 1, 7)
    at(1, y_send, 1, 2, 6)
    at(1, kv_forward, 1)
    at(2, y_send, 1, 3, 5, 4)
    at(3, y_last, 0)
    at(5, y_forward, 1, 0, 1, 7, 2)
    at(7, y_forward, 1, 6, 3, 5, 4)
    at(11, kv_last, 1)
    at(11, y_last, 1)
    at(11, y_reduce, 0, 0, 0)
    at(15, y_reduce, 0, 0, 1)
    at(15, y_reduce, 0, 1, 0)
    at(18, y_reduce, 0, 0, 2)
    at(18, z_out, 0, 0)
    at(18, y_reduce, 0, 1, 1)
    at(22, y_reduce, 0, 1, 2)
    at(22, z_out, 0, 1)
    at(19, y_reduce, 1, 1, 0)
    at(23, y_reduce, 1, 1, 1)
    at(26, y_reduce, 1, 1, 2)
    at(26, z_out, 1, 1)
    at(27, y_reduce, 1, 0, 0)
    at(31, y_reduce, 1, 0, 1)
    at(31, suffix, 1)
    at(31, y_reduce, 1, 0, 2)
    at(31, z_out, 1, 0)
    at(31, finish, 0)
    at(31, finish, 1)

    tile = Tile(0, *order[0])
    for j in range(4):
        tile.front(j)
        if j % 2:
            y_forward(0, *((3, 5), (4,))[j // 2])
    for n in range(len(order)):
        following = Tile(n + 1, *order[n + 1]) if n + 1 < len(order) else None
        for j in range(4):
            if following is not None:
                following.front(j)
            tile.back(j)
            if j == 3:
                tile.store()
                tile = following
            for f, args in events.get(4 * n + j, []):
                f(*args)
    for name in copies:
        if name not in done:
            copy_of(name).wait_recv()
        copy_of(name).wait_send()


def shards(
    queries, block_lists, suffix_lengths, prompt_keys, prompt_values, suffix_keys, suffix_values
):
    hbm = pl.BlockSpec(memory_space=pltpu.HBM)
    vmem = pl.BlockSpec(memory_space=pltpu.VMEM)
    smem = pl.BlockSpec(memory_space=pltpu.SMEM)
    return pl.pallas_call(
        kernel,
        out_shape=jax.ShapeDtypeStruct(queries.shape, bf16),
        in_specs=[hbm, hbm, smem, hbm, hbm, hbm, hbm],
        out_specs=vmem,
        scratch_shapes=[
            pltpu.VMEM(queries.shape, bf16),
            pltpu.VMEM(block_lists.shape, jnp.int32),
            pltpu.VMEM(prompt_keys.shape, bf16),
            pltpu.VMEM(prompt_values.shape, bf16),
            pltpu.VMEM(suffix_keys.shape, bf16),
            pltpu.VMEM(suffix_values.shape, bf16),
            pltpu.VMEM((2, 2, QROWS, 128), bf16),
            pltpu.VMEM((128, 128), f32),
            pltpu.VMEM((2, NY, NZ, 2, QROWS, 128), bf16),
            pltpu.VMEM((2, 4, 2, 2, 2, 128, 128), bf16),
            pltpu.VMEM((2, 2, 2, 128, 128), bf16),
            pltpu.VMEM((TILE, 2048), f32),
            pltpu.VMEM((TILE, 2048), f32),
            pltpu.VMEM((4, 128, 128), bf16),
            pltpu.VMEM((PROWS, 256), bf16),
            pltpu.VMEM((2, NY, NZ, PROWS, 128), bf16),
            pltpu.VMEM((2, 2, 2, PROWS, 128), bf16),
            pltpu.VMEM((2, 2, 2, PROWS, 128), bf16),
            pltpu.VMEM((2, 2, NZ, PROWS, 128), bf16),
            pltpu.VMEM((2, 2, NZ, PROWS, 128), bf16),
            pltpu.VMEM((2, 128, 128), f32),
            pltpu.VMEM((2, 8, 128), f32),
            pltpu.SemaphoreType.DMA((COPIES,)),
            pltpu.SemaphoreType.DMA((COPIES,)),
            pltpu.SemaphoreType.DMA((6,)),
        ],
        compiler_params=pltpu.CompilerParams(
            collective_id=0, has_side_effects=True, vmem_limit_bytes=56 * 1024 * 1024
        ),
    )(queries, block_lists, suffix_lengths, prompt_keys, prompt_values, suffix_keys, suffix_values)


def solution(mesh):
    return jax.shard_map(
        shards,
        mesh=mesh,
        in_specs=(
            P(("ctx", "slab"), None),
            P(("ctx", "slab"), None),
            P(("ctx", "slab")),
            P("ctx", "slab", None),
            P("ctx", "slab", None),
            P(("ctx", "slab"), None, None),
            P(("ctx", "slab"), None, None),
        ),
        out_specs=P(("ctx", "slab"), None),
        check_vma=False,
    )
```

```python
import jax
import jax.numpy as jnp
from jax import lax
from jax.experimental import pallas as pl
from jax.experimental.pallas import tpu as pltpu
from jax.sharding import PartitionSpec as P

HEADS = 64
KV_HEADS = 4
HEAD_DIM = 128
RATIO = HEADS // KV_HEADS
NEG = -1e30
EXP_SCALE = 1.4426950408889634 / HEAD_DIM**0.5

NX, NY, NZ = 4, 4, 8
OWN = 4
ROWS = 64
QROWS = 80
PROWS = 144
TILE = 1024
COPIES = 192


def place(dz):
    return (dz + 1) % NZ


NT = (((1,), (1,)), ((), ()))
TN = (((0,), (0,)), ((), ()))
f32 = jnp.float32
bf16 = jnp.bfloat16


def combine(a, b):
    top_a, top_b = a[128:129], b[128:129]
    top = jnp.maximum(top_a, top_b)
    fa = jnp.exp2((top_a - top) * EXP_SCALE)
    fb = jnp.exp2((top_b - top) * EXP_SCALE)
    values = a[:128] * fa + b[:128] * fb
    total = (a[129:130] + a[130:131]) * fa + (b[129:130] + b[130:131]) * fb
    return values, top, total


def pack(values, top, total):
    high = total.astype(bf16).astype(f32)
    row = lax.broadcasted_iota(jnp.int32, (16, values.shape[1]), 0)
    tail = jnp.where(row == 0, top, jnp.where(row == 1, high, jnp.where(row == 2, total - high, 0.0)))
    return jnp.concatenate([values.astype(bf16), tail.astype(bf16)], axis=0)


def kernel(
    q_hbm, list_hbm, len_in, k_hbm, v_hbm, sk_hbm, sv_hbm, out_ref,
    q_in, list_in, k_in, v_in, sk_in, sv_in, qfmt, work,
    qbuf, kv, vsib, scores0, scores1, hide, eye, part, ra, rb, rc, fin, suf_o, suf_ml,
    send_sems, recv_sems, loc_sems,
):
    ctx = lax.axis_index("ctx")
    slab = lax.axis_index("slab")
    core = lax.rem(ctx, 2)
    z = lax.rem(ctx // 2, NZ)
    x = slab // 2
    y = lax.rem(slab, 2) * 2 + ctx // (2 * NZ)

    def device(x, y, z, core):
        return (lax.rem(y, 2) * NZ + z) * 2 + core, x * 2 + y // 2

    sib = device(x, y, z, 1 - core)
    xps = [device(lax.rem(x + 1, NX), y, z, c) for c in (core, 1 - core)]
    xms = [device(lax.rem(x + NX - 1, NX), y, z, c) for c in (core, 1 - core)]
    yp = device(x, lax.rem(y + 1, NY), z, core)
    ym = device(x, lax.rem(y + NY - 1, NY), z, core)
    along_z = [[device(x, y, lax.rem(z + dz, NZ), c) for dz in range(NZ)] for c in (core, 1 - core)]

    loads = []
    pairs = ((k_hbm, k_in), (v_hbm, v_in), (q_hbm, q_in), (list_hbm, list_in), (sk_hbm, sk_in), (sv_hbm, sv_in))
    for n, (src, dst) in enumerate(pairs):
        loads.append(pltpu.make_async_copy(src, dst, loc_sems.at[n]))
        loads[n].start()

    barrier = pltpu.get_barrier_semaphore()
    peers = [sib, *xps, *xms, yp, ym] + along_z[0][1:] + along_z[1][1:]
    for other in peers:
        pl.semaphore_signal(barrier, inc=1, device_id=other, device_id_type=pl.DeviceIdType.MESH)

    def own_kv(k):
        mine = pl.ds(pl.multiple_of(core * 256 + k * 128, 128), 128)
        theirs = pl.ds(pl.multiple_of((1 - core) * 256 + k * 128, 128), 128)
        for blk in range(2):
            vsib[k, 0, blk] = k_in[blk, :, theirs].T
            vsib[k, 1, blk] = v_in[blk, :, theirs]
            kv[k, 0, 0, 0, blk] = k_in[blk, :, mine].T
            kv[k, 0, 0, 1, blk] = v_in[blk, :, mine]

    loads[0].wait()
    loads[1].wait()
    own_kv(0)

    loads[2].wait()

    def queries(k):
        for half in range(2):
            for h in range(RATIO):
                col = ((half * 2 + k) * RATIO + h) * HEAD_DIM
                work[pl.ds(h * OWN, OWN), :] = q_in[:, col : col + HEAD_DIM].astype(f32)
            qfmt[half, k, 0:ROWS, :] = work[0:ROWS, :].astype(bf16)

    queries(0)
    loads[3].wait()
    lists = list_in[...]
    lane = lax.broadcasted_iota(jnp.int32, (OWN, 128), 1)
    seen = jnp.zeros((OWN, 128), f32)
    for n in range(lists.shape[1]):
        seen = jnp.where(lists[:, n : n + 1] == lane, 1.0, seen)
    work[0:16, :] = jnp.zeros((16, 128), f32)
    work[0:OWN, :] = seen
    for half in range(2):
        qfmt[half, 0, ROWS:QROWS, :] = work[0:16, :].astype(bf16)

    pl.semaphore_wait(barrier, len(peers))

    copies = {}
    done = set()

    def copy_of(name):
        n, src, dst, to = copies[name]
        return pltpu.make_async_remote_copy(
            src_ref=src, dst_ref=dst, send_sem=send_sems.at[n], recv_sem=recv_sems.at[n],
            device_id=to, device_id_type=pl.DeviceIdType.MESH,
        )

    def send(name, src, dst, to):
        copies[name] = (len(copies), src, dst, to)
        copy_of(name).start()

    def got(*name):
        if name not in done:
            done.add(name)
            copy_of(name).wait_recv()

    def kv_send(k):
        for i in range(2):
            send(("kvsib", k, i), vsib.at[k, i], kv.at[k, 0, 1, i], sib)
            for c, src in enumerate((kv.at[k, 0, 0, i], vsib.at[k, i])):
                send(("kv1", k, c, i), src, kv.at[k, 1, c, i], xps[c])
                send(("kv2", k, c, i), src, kv.at[k, 2, c, i], xms[c])

    def kv_forward(k, i):
        got("kv1", k, 0, i)
        send(("kv3", k, 0, i), kv.at[k, 1, 0, i], kv.at[k, 3, 0, i], xps[0])
        got("kv2", k, 1, i)
        send(("kv3", k, 1, i), kv.at[k, 2, 1, i], kv.at[k, 3, 1, i], xms[0])

    def kv_last(k, i):
        got("kvsib", k, i)
        for c in range(2):
            for name in ("kv1", "kv2", "kv3"):
                got(name, k, c, i)

    def slot(k, dy, dz, which):
        rows = pl.ds(0, QROWS if k == 0 else ROWS)
        if which == 2:
            return qbuf.at[k, dy, place(dz), pl.ds(0, 2), rows]
        return qbuf.at[k, dy, place(dz), which, rows]

    def q_send(k):
        end = QROWS if k == 0 else ROWS
        qbuf[k, 0, place(0), 0, 0:end, :] = qfmt[core, k, 0:end, :]
        for to in (0, 1, 7, 2, 6, 3, 5, 4):
            for half in range(2):
                if to or half:
                    src = qfmt.at[core if half == 0 else 1 - core, k, pl.ds(0, end)]
                    send(("q", k, half, -to % NZ), src, slot(k, 0, -to, half), along_z[half][to])

    def y_send(k, *dzs):
        for dz in dzs:
            for half in range(2):
                if dz or half:
                    got("q", k, half, dz)
            send(("y3", k, dz), slot(k, 0, dz, 2), slot(k, 3, dz, 2), yp)
            send(("y1", k, dz), slot(k, 0, dz, 2), slot(k, 1, dz, 2), ym)

    def y_forward(k, *dzs):
        for dz in dzs:
            got("y3", k, dz)
            send(("y2a", k, dz), slot(k, 3, dz, 0), slot(k, 2, dz, 0), yp)
            got("y1", k, dz)
            send(("y2b", k, dz), slot(k, 1, dz, 1), slot(k, 2, dz, 1), ym)

    def y_last(k):
        for dz in range(NZ):
            got("y2a", k, dz)
            got("y2b", k, dz)

    def suffix(k):
        zero = jnp.zeros((ROWS, 128), bf16)
        s = None
        for half in range(2):
            which = core if half == 0 else 1 - core
            cols = pl.ds(pl.multiple_of(which * 256 + k * 128, 128), 128)
            q = qfmt[which, k, 0:ROWS, :]
            q = jnp.concatenate([q, zero] if half == 0 else [zero, q], axis=0)
            keys = sk_in[:, :, cols].reshape(1024, 128)
            more = lax.dot_general(keys, q, NT, preferred_element_type=f32)
            s = more if s is None else s + more
        token = lax.broadcasted_iota(jnp.int32, (1024, 128), 0)
        lane = lax.broadcasted_iota(jnp.int32, (1024, 128), 1)
        branch = lax.broadcasted_iota(jnp.int32, (1, 128), 1) & (OWN - 1)
        length = jnp.zeros((1, 128), jnp.int32)
        for b in range(OWN):
            length = jnp.where(branch == b, len_in[b], length)
        ok = ((token >> 8) == (lane & (OWN - 1))) & ((token & 255) < length)
        top = jnp.max(jnp.where(ok, s, NEG), axis=0, keepdims=True)
        w = jnp.where(ok, jnp.exp2((s - top) * EXP_SCALE), 0.0)
        total = jnp.sum(w, axis=0, keepdims=True)
        w = w.astype(bf16)
        both = []
        for half in range(2):
            which = core if half == 0 else 1 - core
            cols = pl.ds(pl.multiple_of(which * 256 + k * 128, 128), 128)
            values = sv_in[:, :, cols].reshape(1024, 128)
            both.append(lax.dot_general(values, w, TN, preferred_element_type=f32))
        lane = lax.broadcasted_iota(jnp.int32, (128, 128), 1)
        suf_o[k] = jnp.where(lane < ROWS, both[0], both[1])
        suf_ml[k, 0:1] = top
        suf_ml[k, 1:2] = total

    row = lax.broadcasted_iota(jnp.int32, (128, 128), 0)
    lane = lax.broadcasted_iota(jnp.int32, (128, 128), 1)
    block_id = jnp.where(lane < 2, 2 * ctx + lane, 2 * (ctx + 1 - 2 * core) + lane - 2)
    pick = ((row == block_id) & (lane < 4)).astype(f32).astype(bf16)
    row = lax.broadcasted_iota(jnp.int32, (TILE, 256), 0)
    lane = lax.broadcasted_iota(jnp.int32, (TILE, 256), 1)
    spread = ((lane >> 4) == (row >> 6)) & ((lane & 15) == (row & (OWN - 1)))
    spread = spread.astype(f32).astype(bf16)

    def constants():
        row = lax.broadcasted_iota(jnp.int32, (128, 128), 0)
        for j in range(4):
            hide[j] = jnp.where(row == j, NEG, 0.0).astype(bf16)
        row = lax.broadcasted_iota(jnp.int32, (PROWS, 256), 0)
        lane = lax.broadcasted_iota(jnp.int32, (PROWS, 256), 1)
        eye[...] = (row == lane).astype(f32).astype(bf16)

    class Tile:
        def __init__(self, n, k, dys, g):
            self.k, self.dys, self.g = k, dys, g
            self.scores = (scores0, scores1)[n % 2]

        def front(self, j):
            if j == 0:
                slots = slice(4 * self.g, 4 * self.g + 4)
                q = [qbuf[self.k, dy, slots, :, 0:ROWS, :].reshape(TILE // 2, 128) for dy in self.dys]
                q = jnp.concatenate(q, axis=0)
                bits = [qbuf[0, dy, slots, :, ROWS:QROWS, :].reshape(128, 128) for dy in self.dys]
                bits = jnp.concatenate(bits, axis=0)
                unseen = jnp.dot((1.0 - bits.astype(f32)).astype(bf16), pick, preferred_element_type=f32)
                unseen = jnp.dot(spread, unseen.astype(bf16), preferred_element_type=f32)
                self.q = jnp.concatenate([q, unseen.astype(bf16)], axis=1)
                self.top = jnp.full((TILE, 128), NEG, f32)
            keys = jnp.concatenate([kv[self.k, xs, j // 2, 0, j % 2] for xs in range(4)], axis=1)
            keys = jnp.concatenate([keys, jnp.concatenate([hide[j]] * 4, axis=1)], axis=0)
            s = jnp.dot(self.q, keys, preferred_element_type=f32)
            self.scores[:, pl.ds(j * 512, 512)] = s
            for c in range(0, 512, 128):
                self.top = jnp.maximum(self.top, s[:, c : c + 128])

        def back(self, j):
            if j == 0:
                top = jnp.max(self.top, axis=1, keepdims=True)
                self.top = jnp.maximum(top, 0.1 * NEG).astype(bf16).astype(f32)
                self.acc = jnp.zeros((TILE, 256), f32)
            values = jnp.concatenate([kv[self.k, xs, j // 2, 1, j % 2] for xs in range(4)], axis=0)
            values = jnp.concatenate([values, jnp.ones((512, 128), bf16)], axis=1)
            w = jnp.exp2((self.scores[:, pl.ds(j * 512, 512)] - self.top) * EXP_SCALE).astype(bf16)
            self.acc = self.acc + jnp.dot(w, values, preferred_element_type=f32)

        def store(self):
            total = self.acc[:, 128:]
            high = total.astype(bf16).astype(f32)
            lane = lax.broadcasted_iota(jnp.int32, (TILE, 128), 1)
            tail = jnp.where(lane == 0, self.top, jnp.where(lane == 1, high, jnp.where(lane == 2, total - high, 0.0)))
            packed = jnp.concatenate([self.acc[:, :128].astype(bf16), tail.astype(bf16)], axis=1)
            turned = lax.dot_general(eye[...], packed, NT, preferred_element_type=f32).astype(bf16)
            for i in range(8):
                part[self.k, self.dys[i // 4], 4 * self.g + i % 4] = turned[:, i * 128 : i * 128 + 128]

    def fold(pieces):
        total = pieces[0].astype(f32)
        row = lax.broadcasted_iota(jnp.int32, (16, 128), 0)
        for other in pieces[1:-1]:
            values, top, mass = combine(total, other.astype(f32))
            tail = jnp.where(row == 0, top, jnp.where(row == 1, mass, 0.0))
            total = jnp.concatenate([values, tail], axis=0)
        return combine(total, pieces[-1].astype(f32))

    def merge(k, dy, dz, *others):
        dz = place(dz)
        others = [buf[tuple(index)] for buf, *index in others]
        part[k, dy, dz] = pack(*fold([part[k, dy, dz]] + others))

    def y_reduce(k, g, step):
        dzs = [(4 * g + i - 1) % NZ for i in range(4)]
        a, b = pl.ds(4 * g, 2), pl.ds(4 * g + 2, 2)
        if step == 0:
            send(("ra", k, g), part.at[k, 2, a], ra.at[k, g], yp)
            send(("rb", k, g), part.at[k, 2, b], rb.at[k, g], ym)
            send(("rcb", k, g), part.at[k, 1, b], rc.at[k, 0, b], yp)
        elif step == 1:
            send(("rda", k, g), part.at[k, 3, a], rc.at[k, 1, a], ym)
            got("ra", k, g)
            for i in range(2):
                merge(k, 1, dzs[i], (ra, k, g, i))
            send(("rca", k, g), part.at[k, 1, a], rc.at[k, 0, a], yp)
            got("rb", k, g)
            for i in range(2):
                merge(k, 3, dzs[2 + i], (rb, k, g, i))
            send(("rdb", k, g), part.at[k, 3, b], rc.at[k, 1, b], ym)
        else:
            for name in ("rcb", "rda", "rca", "rdb"):
                got(name, k, g)
            for i in (1, 2, 0, 3) if g else (3, 0, 2, 1):
                merge(k, 0, dzs[i], (rc, k, 0, 4 * g + i), (rc, k, 1, 4 * g + i))

    def z_out(k, g):
        for dz in [(4 * g + i - 1) % NZ for i in range(4)]:
            for half in range(2):
                if dz or half:
                    send(("fin", k, half, dz), part.at[k, 0, place(dz)], fin.at[k, half, dz], along_z[half][dz])

    def finish(k):
        lane = lax.broadcasted_iota(jnp.int32, (PROWS, 128), 1)
        pieces = []
        for dz in range(NZ):
            for half in range(2):
                if dz or half:
                    got("fin", k, half, dz)
            first = fin[k, 0, dz] if dz else part[k, 0, place(0)]
            pieces.append(jnp.where(lane < ROWS, first.astype(f32), fin[k, 1, dz].astype(f32)))
        values, top_a, mass = fold(pieces)
        top_b = suf_ml[k, 0:1]
        top = jnp.maximum(top_a, top_b)
        fa = jnp.exp2((top_a - top) * EXP_SCALE)
        fb = jnp.exp2((top_b - top) * EXP_SCALE)
        total = mass * fa + suf_ml[k, 1:2] * fb
        work[...] = ((values * fa + suf_o[k] * fb) / total).T
        for half in range(2):
            which = core if half == 0 else 1 - core
            for h in range(RATIO):
                col = pl.multiple_of((which * 2 + k) * RATIO * HEAD_DIM + h * HEAD_DIM, 128)
                rows = work[pl.ds(half * ROWS + h * OWN, OWN), :]
                out_ref[:, pl.ds(col, HEAD_DIM)] = rows.astype(bf16)

    kv_send(0)
    q_send(0)
    own_kv(1)
    y_send(0, 0)
    kv_forward(0, 0)
    queries(1)
    y_send(0, 1, 7, 2, 6)
    kv_forward(0, 1)
    y_send(0, 3, 5, 4)
    kv_send(1)
    q_send(1)
    constants()
    y_forward(0, 0, 1, 7, 2)
    loads[4].wait()
    loads[5].wait()
    kv_last(0, 0)

    order = [(0, dys, g) for dys in ((0, 1), (3, 2)) for g in (0, 1)]
    order += [(1, dys, g) for g in (1, 0) for dys in ((2, 1), (3, 0))]
    events = {}

    def at(n, f, *args):
        events.setdefault(n, []).append((f, args))

    at(0, y_send, 1, 0, 1, 7)
    at(1, y_send, 1, 2, 6)
    at(1, kv_forward, 1, 0)
    at(2, kv_forward, 1, 1)
    at(2, y_send, 1, 3, 5, 4)
    at(3, y_last, 0)
    at(5, y_forward, 1, 0, 1, 7, 2)
    at(7, y_forward, 1, 6, 3, 5, 4)
    at(11, kv_last, 1, 0)
    at(11, kv_last, 1, 1)
    at(11, y_last, 1)
    at(11, y_reduce, 0, 0, 0)
    at(15, y_reduce, 0, 0, 1)
    at(15, y_reduce, 0, 1, 0)
    at(18, y_reduce, 0, 0, 2)
    at(18, z_out, 0, 0)
    at(18, y_reduce, 0, 1, 1)
    at(22, y_reduce, 0, 1, 2)
    at(22, z_out, 0, 1)
    at(19, y_reduce, 1, 1, 0)
    at(23, y_reduce, 1, 1, 1)
    at(26, y_reduce, 1, 1, 2)
    at(26, z_out, 1, 1)
    at(27, y_reduce, 1, 0, 0)
    at(31, y_reduce, 1, 0, 1)
    at(31, suffix, 0)
    at(31, y_reduce, 1, 0, 2)
    at(31, z_out, 1, 0)
    at(31, suffix, 1)
    at(31, finish, 0)
    at(31, finish, 1)

    tile = Tile(0, *order[0])
    for j in range(4):
        tile.front(j)
        if j == 1:
            y_forward(0, 6, 3)
    y_forward(0, 5, 4)
    kv_last(0, 1)
    for n in range(len(order)):
        following = Tile(n + 1, *order[n + 1]) if n + 1 < len(order) else None
        for j in range(4):
            if following is not None:
                following.front(j)
            tile.back(j)
            if j == 3:
                tile.store()
                tile = following
            for f, args in events.get(4 * n + j, []):
                f(*args)
    for name in copies:
        if name not in done:
            copy_of(name).wait_recv()
        copy_of(name).wait_send()


def shards(
    queries, block_lists, suffix_lengths, prompt_keys, prompt_values, suffix_keys, suffix_values
):
    hbm = pl.BlockSpec(memory_space=pltpu.HBM)
    vmem = pl.BlockSpec(memory_space=pltpu.VMEM)
    smem = pl.BlockSpec(memory_space=pltpu.SMEM)
    return pl.pallas_call(
        kernel,
        out_shape=jax.ShapeDtypeStruct(queries.shape, bf16),
        in_specs=[hbm, hbm, smem, hbm, hbm, hbm, hbm],
        out_specs=vmem,
        scratch_shapes=[
            pltpu.VMEM(queries.shape, bf16),
            pltpu.VMEM(block_lists.shape, jnp.int32),
            pltpu.VMEM(prompt_keys.shape, bf16),
            pltpu.VMEM(prompt_values.shape, bf16),
            pltpu.VMEM(suffix_keys.shape, bf16),
            pltpu.VMEM(suffix_values.shape, bf16),
            pltpu.VMEM((2, 2, QROWS, 128), bf16),
            pltpu.VMEM((128, 128), f32),
            pltpu.VMEM((2, NY, NZ, 2, QROWS, 128), bf16),
            pltpu.VMEM((2, 4, 2, 2, 2, 128, 128), bf16),
            pltpu.VMEM((2, 2, 2, 128, 128), bf16),
            pltpu.VMEM((TILE, 2048), f32),
            pltpu.VMEM((TILE, 2048), f32),
            pltpu.VMEM((4, 128, 128), bf16),
            pltpu.VMEM((PROWS, 256), bf16),
            pltpu.VMEM((2, NY, NZ, PROWS, 128), bf16),
            pltpu.VMEM((2, 2, 2, PROWS, 128), bf16),
            pltpu.VMEM((2, 2, 2, PROWS, 128), bf16),
            pltpu.VMEM((2, 2, NZ, PROWS, 128), bf16),
            pltpu.VMEM((2, 2, NZ, PROWS, 128), bf16),
            pltpu.VMEM((2, 128, 128), f32),
            pltpu.VMEM((2, 8, 128), f32),
            pltpu.SemaphoreType.DMA((COPIES,)),
            pltpu.SemaphoreType.DMA((COPIES,)),
            pltpu.SemaphoreType.DMA((6,)),
        ],
        compiler_params=pltpu.CompilerParams(
            collective_id=0, has_side_effects=True, vmem_limit_bytes=56 * 1024 * 1024
        ),
    )(queries, block_lists, suffix_lengths, prompt_keys, prompt_values, suffix_keys, suffix_values)


def solution(mesh):
    return jax.shard_map(
        shards,
        mesh=mesh,
        in_specs=(
            P(("ctx", "slab"), None),
            P(("ctx", "slab"), None),
            P(("ctx", "slab")),
            P("ctx", "slab", None),
            P("ctx", "slab", None),
            P(("ctx", "slab"), None, None),
            P(("ctx", "slab"), None, None),
        ),
        out_specs=P(("ctx", "slab"), None),
        check_vma=False,
    )
```
